128 devices in a mesh: ctx: 16 (over z, x_hi, core), exp: 8 (over y, x_lo).
Axes of the slice: x: 4 (x_hi: 2, x_lo: 2; x = x_hi * 2 + x_lo), y: 4, z: 4, core: 2. Of those that a mesh axis runs over, the one named last changes fastest.
Arguments:
- stream: bfloat16 [2048, 6144], P(('ctx', 'exp')), may hold values from -3 to 3
- queries: bfloat16 [2048, 8192], P('ctx', 'exp'), may hold values from -6 to 6
- key_head_rows: bfloat16 [2048, 1024], P('ctx', 'exp'), may hold values from -6 to 6
- value_head_rows: bfloat16 [2048, 1024], P('ctx', 'exp'), may hold values from -6 to 6
- block_order: int32 [32], replicated, may hold values from 0 to 31, each once
- out_weight: bfloat16 [8192, 6144], P('exp', 'ctx'), may hold values from -0.5 to 0.5
- norm_gain: float32 [6144], replicated, may hold values from 0.5 to 1.5
- gate_weight: bfloat16 [8, 6144, 6144], P('exp', None, 'ctx'), may hold values from -0.078125 to 0.078125
- up_weight: bfloat16 [8, 6144, 6144], P('exp', None, 'ctx'), may hold values from -0.078125 to 0.078125
- down_weight: bfloat16 [8, 6144, 6144], P('exp', 'ctx'), may hold values from -0.078125 to 0.078125
- expert_ids: int32 [2048, 2], P(('ctx', 'exp')), may hold values from 0 to 7, all different within a row; in each aligned block of 16 rows (0 to 15, 16 to 31, ...) at most 8 rows name the same one
- expert_weights: float32 [2048, 2], P(('ctx', 'exp')), may hold values from 0.2 to 1
Outputs:
- attended: bfloat16 [2048, 6144], P(('ctx', 'exp'))
- mixed: bfloat16 [2048, 6144], P(('ctx', 'exp'))
The draws below stay inside these ranges and needn't reach their ends.
Inputs may be any that keep to these rules, and one draw needn't show every extreme that they name: `expert_ids`: in each aligned block of 16 rows no expert is named by more than 8 rows, a bound that some block reaches; the two experts of a row differ. `block_order`: A permutation of the stored half-blocks of 64 rows.
All inputs are finite; a program needn't handle non-finite values.
Results may differ from the reference program's by a relative error of at most 0.025.
Values may be sent and summed in bfloat16 or wider, within the bound.
A program may use at most 128 MiB of HBM per device.

```python
import math
import jax
import jax.numpy as jnp
import numpy as np
from jax import lax

D = 6144
QUERY_HEADS = 64
KEY_VALUE_HEADS = 8
PER_LANE_DIM = 128
FF = 6144
SEQUENCE_TOKENS = 2048
BLOCK = 64
MOE_DEV = 16
EXPERTS = 8
CAP = 8
FF_DEV = 384
N_CTX = 16


def draw_queries(key, part):
    key = jax.random.fold_in(key, 11)
    final_result = jnp.clip(jax.random.normal(key, (SEQUENCE_TOKENS, QUERY_HEADS * PER_LANE_DIM)), -6.0, 6.0)
    return final_result.astype(jnp.bfloat16)


def draw_key_head_rows(key, part):
    key = jax.random.fold_in(key, 23)
    final_result = jnp.clip(jax.random.normal(key, (SEQUENCE_TOKENS, KEY_VALUE_HEADS * PER_LANE_DIM)), -6.0, 6.0)
    return final_result.astype(jnp.bfloat16)


def steps_of(key, extent, cuts, smallest, largest):
    def one(position, blocks):
        steps = jax.random.uniform(jax.random.fold_in(jax.random.fold_in(key, 6), position), (blocks,), jnp.float32, smallest / len(cuts), largest / len(cuts))
        return jnp.repeat(jnp.exp(steps), extent[position] // blocks).reshape((-1,) + (1,) * (len(extent) - position - 1))

    factor_of = one(*cuts[0])
    for cut in cuts[1:]:
        factor_of = factor_of * one(*cut)
    return factor_of


def deal_out(stream_key, own, number, rows, count, top, most, skew):
    ranking = jax.random.permutation(stream_key, count)
    heavy_load, usual = load_shares(count, rows * top, most, skew, True), load_shares(count, rows * top, most, skew, False)
    places = jnp.arange(count)

    def named(tallies, turn):
        used = int((tallies > 0).sum())
        fixed = max(1, used // 4)
        shifted = fixed + (places - fixed + turn * (used - fixed)) % max(1, count - fixed)
        return jnp.zeros((count,), jnp.int32).at[ranking[jnp.where(places < fixed, places, shifted)]].set(jnp.asarray(tallies, jnp.int32))

    tallies = jnp.where(number % 4 == 0, named(heavy_load, number // 4), named(usual, number - number // 4 - 1))
    mixed = jax.random.permutation(jax.random.fold_in(own, 3), count)
    giver, receiver = mixed[0:count // 2 * 2:2], mixed[1:count // 2 * 2:2]
    slack = jnp.minimum(tallies[giver] - 1, most - tallies[receiver]) // 2
    slack = jnp.where((giver == ranking[0]) | (receiver == ranking[0]) | (tallies[receiver] == 0), 0, jnp.maximum(slack, 0))
    shifted = jax.random.randint(jax.random.fold_in(own, 4), (count // 2,), 0, 1 << 20) % (slack + 1)
    tallies = tallies.at[giver].add(-shifted).at[receiver].add(shifted)
    labels = jnp.searchsorted(jnp.cumsum(tallies), jnp.arange(rows * top), side="right").astype(jnp.int32)
    listing = labels.reshape(top, rows).T
    listing = listing[jax.random.permutation(jax.random.fold_in(own, 1), rows)]
    turn = jax.random.randint(jax.random.fold_in(own, 2), (rows, 1), 0, top)
    return jnp.take_along_axis(listing, (jnp.arange(top)[None, :] + turn) % top, axis=1)


def load_shares(amount, total, reach, skew, full):
    portions = [(1 << 20) // math.isqrt(rank ** skew) + 1 for rank in range(1, amount + 1)]
    largest = reach if full else min(reach, max(-(-total // amount), total * portions[0] // sum(portions)))
    least = 1 if total - largest >= amount - 1 else 0
    holding, rest = [largest] + [least] * (amount - 1), total - largest - least * (amount - 1)
    while rest > 0:
        movable = [i for i in range(1, amount) if holding[i] < largest] or [i for i in range(1, amount) if holding[i] < reach]
        mass, left = sum([portions[i] for i in movable]), rest
        for i in movable:
            addition = min(reach - holding[i], max(1, left * portions[i] // mass), rest)
            holding[i] = holding[i] + addition
            rest = rest - addition
    return np.array(holding)


def scatter_about(key, shape, deviation, reach, cuts=(), kind=jnp.bfloat16):
    loudness = steps_of(key, shape, cuts, -0.22, 0.18) if cuts else 1.0
    values = jax.random.normal(key, shape, jnp.float32) * deviation * loudness
    return jnp.minimum(jnp.maximum(values, -reach), reach).astype(kind)


def setup_inputs(seed: int = 0) -> dict:
    key_of = jax.random.split(jax.random.key(seed), 13)
    stream = scatter_about(key_of[0], (SEQUENCE_TOKENS, D), 0.5, 3.0, ((0, 128),))
    queries = draw_queries(jax.random.fold_in(key_of[12], 71), 0)
    key_head_rows = draw_key_head_rows(jax.random.fold_in(key_of[12], 71), 0)
    value_head_rows = scatter_about(key_of[3], (SEQUENCE_TOKENS, KEY_VALUE_HEADS * PER_LANE_DIM), 1.0, 6.0, ((0, 16), (1, 8)))
    block_order = jax.random.permutation(key_of[4], SEQUENCE_TOKENS // BLOCK).astype(jnp.int32)
    out_weight = scatter_about(key_of[5], (QUERY_HEADS * PER_LANE_DIM, D), PER_LANE_DIM ** -0.5, 0.5, ((0, 8), (1, 16)))
    norm_gain = jnp.clip(jax.random.uniform(key_of[6], (D,), jnp.float32, 0.5, 1.5), 0.5, 1.5)
    gate_weight = scatter_about(key_of[7], (EXPERTS, D, FF), D ** -0.5, 0.078125, ((0, 8), (2, 16)))
    up_weight = scatter_about(key_of[8], (EXPERTS, D, FF), D ** -0.5, 0.078125, ((0, 8), (2, 16)))
    down_weight = scatter_about(key_of[9], (EXPERTS, FF, D), FF ** -0.5, 0.078125, ((0, 8), (1, 16)))
    expert_ids_keys = jax.random.split(jax.random.fold_in(key_of[10], 1), SEQUENCE_TOKENS // MOE_DEV)
    expert_ids_turns = jax.random.permutation(jax.random.fold_in(key_of[10], 3), SEQUENCE_TOKENS // MOE_DEV)
    expert_ids = jax.vmap(lambda own, number: deal_out(jax.random.fold_in(key_of[10], 2), own, number, MOE_DEV, EXPERTS, 2, CAP, 2))(expert_ids_keys, expert_ids_turns).reshape((SEQUENCE_TOKENS, 2))
    expert_weights = jnp.clip(0.2 + 0.8 * jax.random.uniform(key_of[11], (SEQUENCE_TOKENS, 2), jnp.float32) ** steps_of(key_of[11], (SEQUENCE_TOKENS, 2), ((0, 128),), -0.2, 0.2), 0.2, 1.0)
    return dict(stream=stream, queries=queries, key_head_rows=key_head_rows, value_head_rows=value_head_rows, block_order=block_order, out_weight=out_weight, norm_gain=norm_gain, gate_weight=gate_weight, up_weight=up_weight, down_weight=down_weight, expert_ids=expert_ids, expert_weights=expert_weights)


def stored_positions(block_order):
    rows = jnp.arange(SEQUENCE_TOKENS, dtype=jnp.int32)
    return block_order[rows // BLOCK] * BLOCK + rows % BLOCK

def reference(stream, queries, key_head_rows, value_head_rows, block_order, out_weight, norm_gain, gate_weight, up_weight, down_weight, expert_ids, expert_weights):
    positions = stored_positions(block_order)
    visible = positions[None, :] <= positions[:, None]
    head_group = QUERY_HEADS // KEY_VALUE_HEADS
    heads_of_query = queries.reshape(SEQUENCE_TOKENS, KEY_VALUE_HEADS, head_group, PER_LANE_DIM).transpose(1, 0, 2, 3)
    heads_of_key = key_head_rows.reshape(SEQUENCE_TOKENS, KEY_VALUE_HEADS, PER_LANE_DIM).transpose(1, 0, 2)
    heads_of_value = value_head_rows.reshape(SEQUENCE_TOKENS, KEY_VALUE_HEADS, PER_LANE_DIM).transpose(1, 0, 2)

    def one_head(operands):
        asking_tile_entries, lookup_tile_entries, value_block_rows = operands
        similarity_logits = jnp.einsum('pgj,qj->gpq', asking_tile_entries.astype(jnp.float32), lookup_tile_entries.astype(jnp.float32)) * PER_LANE_DIM ** (-0.5)
        similarity_logits = jnp.where(visible[None], similarity_logits, -1e+30)
        peak = lax.optimization_barrier(jnp.max(similarity_logits, axis=-1, keepdims=True))
        expd = jnp.where(visible[None], jnp.exp(similarity_logits - peak), 0.0)
        total = lax.optimization_barrier(jnp.sum(expd, axis=-1))
        probabilities = expd.astype(jnp.bfloat16)
        summed_output = jnp.einsum('lhs,sn->lhn', probabilities.astype(jnp.float32), value_block_rows.astype(jnp.float32))
        return (summed_output / total[..., None]).astype(jnp.bfloat16)
    outputs = lax.map(one_head, (heads_of_query, heads_of_key, heads_of_value))
    heads_out = outputs.transpose(2, 0, 1, 3).reshape(SEQUENCE_TOKENS, QUERY_HEADS * PER_LANE_DIM)
    attended_wide = stream.astype(jnp.float32) + jnp.dot(heads_out, out_weight, preferred_element_type=jnp.float32)
    attended = attended_wide.astype(jnp.bfloat16)
    widened = attended.astype(jnp.float32)
    normed = (widened * lax.rsqrt(lax.optimization_barrier(jnp.mean(widened * widened, axis=-1, keepdims=True)) + 1e-05) * norm_gain).astype(jnp.bfloat16)
    most_rows = SEQUENCE_TOKENS // MOE_DEV * CAP

    def one_expert(carry, operands):
        expert, gate_block, up_block, contract_matrix_part = operands
        routed_weight = lax.optimization_barrier(jnp.sum(jnp.where(expert_ids == expert, expert_weights, 0.0), axis=1))
        excluded_region = jnp.where(jnp.any(expert_ids == expert, axis=1), 0, 1).astype(jnp.int32)
        order = jnp.argsort(excluded_region, stable=True)[:most_rows].astype(jnp.int32)
        picked = normed[order]
        gate_part = jnp.dot(picked, gate_block, preferred_element_type=jnp.float32)
        up_part = jnp.dot(picked, up_block, preferred_element_type=jnp.float32)
        hidden = (jax.nn.silu(gate_part) * up_part).astype(jnp.bfloat16)

        def one_group(acc, group_index):
            start = (group_index * FF_DEV).astype(jnp.int32)
            piece = lax.dynamic_slice_in_dim(hidden, start, FF_DEV, 1)
            weights = lax.dynamic_slice_in_dim(contract_matrix_part, start, FF_DEV, 0)
            term = jnp.dot(piece, weights, preferred_element_type=jnp.float32).astype(jnp.bfloat16)
            term = lax.optimization_barrier(term)
            return (acc + term.astype(jnp.float32), None)
        group_sum, _ = lax.scan(one_group, jnp.zeros((most_rows, D), jnp.float32), jnp.arange(N_CTX, dtype=jnp.int32))
        expert_out = group_sum.astype(jnp.bfloat16)
        contribution = expert_out.astype(jnp.float32) * routed_weight[order][:, None]
        return (carry.at[order].add(contribution), None)
    combined, _ = lax.scan(one_expert, jnp.zeros((SEQUENCE_TOKENS, D), jnp.float32), (jnp.arange(EXPERTS, dtype=jnp.int32), gate_weight, up_weight, down_weight))
    mixed = (attended.astype(jnp.float32) + combined).astype(jnp.bfloat16)
    return (attended, mixed)
```

```python
import functools

import jax
import jax.numpy as jnp
from jax import lax
from jax.experimental import pallas as pl
from jax.experimental.pallas import tpu as pltpu
from jax.sharding import PartitionSpec as P

PER_LANE_DIM = 128
MESH = pl.DeviceIdType.MESH
VMEM_LIMIT = 60 * 2**20
NC = 4


def place():
    ctx = lax.axis_index("ctx")
    exp = lax.axis_index("exp")
    return ctx // 4, lax.rem(ctx // 2, 2), lax.rem(ctx, 2), exp


def remote(src, dst, send, recv, device):
    return pltpu.make_async_remote_copy(
        src_ref=src, dst_ref=dst, send_sem=send, recv_sem=recv, device_id=device, device_id_type=MESH
    )


def greet(devices):
    barrier = pltpu.get_barrier_semaphore()
    for device in devices:
        pl.semaphore_signal(barrier, inc=1, device_id=device, device_id_type=MESH)
    pl.semaphore_wait(barrier, len(devices))


def slot_match(meta, core):
    row = lax.broadcasted_iota(jnp.int32, (128, 128), 0)
    lane = lax.broadcasted_iota(jnp.int32, (128, 128), 1)
    expert = (row // 16).astype(jnp.float32)
    first = (meta[0:1, :] == expert) & (lane < 16)
    second = (meta[1:2, :] == expert) & (lane < 16)
    named = jnp.where(first | second, 1.0, 0.0)
    earlier = jnp.where(row < lane, 1.0, 0.0)
    rank = jnp.dot(
        named.astype(jnp.bfloat16), earlier.astype(jnp.bfloat16), preferred_element_type=jnp.float32
    )
    slot = lax.rem(row, 8).astype(jnp.float32)
    mine = lax.rem(row // 8, 2) == core
    match = jnp.where((rank == slot) & mine, named, 0.0)
    weight = match * jnp.where(first, meta[2:3, :], meta[3:4, :])
    return match[:, :16].astype(jnp.bfloat16), weight.T[:16, :]


def experts_kernel(
    att_ref, gain_ref, meta_ref, gate_ref, up_ref, down_ref, out_ref,
    wgu, wd, meta_sib, nrm, nsib, disp, rows, rows_sib, acc, hid, part,
    got1, got2, got3, got4, got5, final, back, contrib, contrib_sib,
    load_sem, pre_s, pre_r, disp_s, disp_r, ga_s, ga_r, sib_s, sib_r, hid_s, hid_r, rs_s, rs_r, back_s, back_r,
):
    z, xh, core, exp = place()
    width = rows.shape[-1]
    half = NC * width
    up_z, down_z, far_z = lax.rem(z + 1, 4), lax.rem(z + 3, 4), lax.rem(z + 2, 4)

    def dev(a, b, c=None, e=None):
        return (a * 4 + b * 2 + (core if c is None else c), exp if e is None else e)

    def blk(a, b):
        return a * 2 + b

    zp, zm, xp, sib = dev(up_z, xh), dev(down_z, xh), dev(z, 1 - xh), dev(z, xh, 1 - core)
    peers = [lax.rem(exp + j, 8) for j in range(1, 8)]
    own_block = blk(z, xh)

    loads = [
        pltpu.make_async_copy(gate_ref.at[0], wgu.at[:, pl.ds(0, 384)], load_sem.at[0]),
        pltpu.make_async_copy(up_ref.at[0], wgu.at[:, pl.ds(384, 384)], load_sem.at[1]),
        pltpu.make_async_copy(
            down_ref.at[0, :, pl.ds(pl.multiple_of(core * half, 128), half)],
            wd.at[pl.ds(pl.multiple_of(core * 384, 128), 384)],
            load_sem.at[2],
        ),
    ]
    for load in loads:
        load.start()
    greet([zp, zm, xp, sib] + [dev(z, xh, None, e) for e in peers])

    send_meta = remote(meta_ref, meta_sib, pre_s.at[0], pre_r.at[0], sib)
    send_meta.start()
    wide = att_ref[...].astype(jnp.float32)
    normed = (
        wide * lax.rsqrt(jnp.mean(wide * wide, axis=-1, keepdims=True) + 1e-05) * gain_ref[...]
    ).astype(jnp.bfloat16)
    nrm[0] = normed[:, :half]
    nrm[1] = normed[:, half:]
    send_nrm = remote(nrm.at[1 - core], nsib, pre_s.at[1], pre_r.at[1], sib)
    send_nrm.start()
    match_own, weight_own = slot_match(meta_ref[...], core)
    send_meta.wait_recv()
    match_sib, weight_sib = slot_match(meta_sib[...], 1 - core)
    send_nrm.wait_recv()

    dispatches = []
    for c in range(NC):
        cols = pl.ds(c * width, width)
        picked = jnp.dot(match_own, nrm[core, :, cols], preferred_element_type=jnp.float32) + jnp.dot(
            match_sib, nsib[:, cols], preferred_element_type=jnp.float32
        )
        disp[c] = picked.astype(jnp.bfloat16).reshape(8, 16, width)
        sends = []
        for j, e in enumerate(peers):
            copy = remote(
                disp.at[c, e], rows.at[c, own_block, exp], disp_s.at[c, j], disp_r.at[c, j],
                dev(z, xh, None, e),
            )
            copy.start()
            sends.append(copy)
        rows[c, own_block, exp] = disp[c, exp]
        dispatches.append(sends)
    send_down = remote(
        down_ref.at[0, :, pl.ds(pl.multiple_of((1 - core) * half, 128), half)],
        wd.at[pl.ds(pl.multiple_of(core * 384, 128), 384)],
        pre_s.at[2], pre_r.at[2], sib,
    )
    send_down.start()

    gather = [[None] * 8 for _ in range(NC)]
    shares = [[] for _ in range(NC)]

    def forward(c, k, block, device, part_of=None):
        ref = rows.at[c, block] if part_of is None else rows.at[c, block, pl.ds(part_of * 4, 4)]
        gather[c][k] = remote(ref, ref, ga_s.at[c, k], ga_r.at[c, k], device)
        gather[c][k].start()

    def share(c, block):
        j = len(shares[c])
        copy = remote(rows.at[c, block], rows_sib.at[c, block], sib_s.at[c, j], sib_r.at[c, j], sib)
        copy.start()
        shares[c].append(copy)

    def gather_a(c):
        for copy in dispatches[c]:
            copy.wait_recv()
        forward(c, 0, own_block, zp)
        forward(c, 1, own_block, zm)
        forward(c, 2, own_block, xp)
        share(c, own_block)

    def gather_b(c):
        gather[c][0].wait_recv()
        forward(c, 3, blk(down_z, xh), zp, 0)
        share(c, blk(down_z, xh))
        gather[c][1].wait_recv()
        forward(c, 4, blk(up_z, xh), zm, 1)
        share(c, blk(up_z, xh))
        gather[c][2].wait_recv()
        forward(c, 5, blk(z, 1 - xh), zp)
        forward(c, 6, blk(z, 1 - xh), zm)
        share(c, blk(z, 1 - xh))

    def gather_c(c):
        gather[c][3].wait_recv()
        gather[c][4].wait_recv()
        forward(c, 7, blk(far_z, xh), xp)
        share(c, blk(far_z, xh))

    def gather_d(c):
        gather[c][5].wait_recv()
        share(c, blk(down_z, 1 - xh))
        gather[c][6].wait_recv()
        share(c, blk(up_z, 1 - xh))
        gather[c][7].wait_recv()
        share(c, blk(far_z, 1 - xh))

    def multiply(source, c, first_col, fresh):
        base = pl.multiple_of(first_col + c * width, 128)

        def body(i, carry):
            lhs = source[c, pl.ds(i * 2, 2)].reshape(256, width)
            term = jnp.dot(lhs, wgu[pl.ds(base, width), :], preferred_element_type=jnp.float32)
            if fresh:
                acc[i] = term
            else:
                acc[i] += term
            return carry

        lax.fori_loop(0, 4, body, 0)

    def multiply_own(c):
        if c == 0:
            loads[0].wait()
            loads[1].wait()
        multiply(rows, c, core * half, c == 0)

    def multiply_sib(c):
        for copy in shares[c]:
            copy.wait_recv()
        multiply(rows_sib, c, (1 - core) * half, False)

    gather_a(0)
    gather_a(1)
    gather_b(0)
    gather_c(0)
    gather_a(2)
    gather_b(1)
    gather_d(0)
    multiply_own(0)
    gather_c(1)
    gather_a(3)
    gather_b(2)
    gather_d(1)
    multiply_sib(0)
    gather_c(2)
    multiply_own(1)
    gather_b(3)
    gather_d(2)
    multiply_sib(1)
    gather_c(3)
    multiply_own(2)
    multiply_sib(2)
    gather_d(3)
    multiply_own(3)
    multiply_sib(3)

    mine = pl.ds(pl.multiple_of(core * 384, 128), 384)
    sent_hidden = []
    for i in range(4):
        gate_part = acc[i, :, :384]
        up_part = acc[i, :, 384:]
        hid[i, :, mine] = (gate_part / (1.0 + jnp.exp(-gate_part)) * up_part).astype(jnp.bfloat16)
        copy = remote(hid.at[i, :, mine], hid.at[i, :, mine], hid_s.at[i], hid_r.at[i], sib)
        copy.start()
        sent_hidden.append(copy)
    loads[2].wait()
    send_down.wait_recv()
    for copy in sent_hidden:
        copy.wait_recv()

    reduce = [[None] * 8 for _ in range(NC)]
    returns = []

    def send_sum(c, k, src, dst, device):
        reduce[c][k] = remote(src, dst, rs_s.at[c, k], rs_r.at[c, k], device)
        reduce[c][k].start()

    def f32(value):
        return value.astype(jnp.float32)

    def reduce_a(c):
        def body(i, carry):
            out = jnp.dot(hid[i], wd[:, c * width : (c + 1) * width], preferred_element_type=jnp.float32)
            part[c, pl.ds(i * 2, 2)] = out.astype(jnp.bfloat16).reshape(2, 8, 16, width)
            return carry

        lax.fori_loop(0, 4, body, 0)
        send_sum(c, 0, part.at[c, blk(up_z, 1 - xh)], got1.at[c, 0], zp)
        send_sum(c, 1, part.at[c, blk(down_z, 1 - xh)], got1.at[c, 1], zm)
        send_sum(c, 2, part.at[c, blk(far_z, 1 - xh)], got2.at[c], xp)

    def reduce_b(c):
        reduce[c][2].wait_recv()
        block = blk(far_z, xh)
        part[c, block] = (f32(part[c, block]) + f32(got2[c])).astype(jnp.bfloat16)
        send_sum(c, 3, part.at[c, block, pl.ds(0, 4)], got4.at[c, 0], zm)
        send_sum(c, 4, part.at[c, block, pl.ds(4, 4)], got4.at[c, 1], zp)
        reduce[c][0].wait_recv()
        reduce[c][1].wait_recv()
        block = blk(z, 1 - xh)
        part[c, block] = (f32(part[c, block]) + f32(got1[c, 0]) + f32(got1[c, 1])).astype(jnp.bfloat16)
        send_sum(c, 5, part.at[c, block], got3.at[c], xp)

    def reduce_c(c):
        reduce[c][3].wait_recv()
        block = blk(down_z, xh)
        part[c, block, 0:4] = (f32(part[c, block, 0:4]) + f32(got4[c, 0])).astype(jnp.bfloat16)
        send_sum(c, 6, part.at[c, block], got5.at[c, 0], zm)
        reduce[c][4].wait_recv()
        block = blk(up_z, xh)
        part[c, block, 4:8] = (f32(part[c, block, 4:8]) + f32(got4[c, 1])).astype(jnp.bfloat16)
        send_sum(c, 7, part.at[c, block], got5.at[c, 1], zp)

    def reduce_d(c):
        reduce[c][5].wait_recv()
        reduce[c][6].wait_recv()
        reduce[c][7].wait_recv()
        final[c] = (
            f32(part[c, own_block]) + f32(got3[c]) + (f32(got5[c, 0]) + f32(got5[c, 1]))
        ).astype(jnp.bfloat16)
        sends = []
        for j, e in enumerate(peers):
            copy = remote(
                final.at[c, e], back.at[c, exp], back_s.at[c, j], back_r.at[c, j], dev(z, xh, None, e)
            )
            copy.start()
            sends.append(copy)
        back[c, exp] = final[c, exp]
        returns.append(sends)

    def combine(c):
        for copy in returns[c]:
            copy.wait_recv()
        values = f32(back[c].reshape(128, width))
        contrib_sib[:, c * width : (c + 1) * width] = jnp.dot(
            weight_sib, values, precision=lax.Precision.HIGHEST, preferred_element_type=jnp.float32
        )
        total = jnp.dot(
            weight_own, values, precision=lax.Precision.HIGHEST, preferred_element_type=jnp.float32
        )
        cols = pl.ds(pl.multiple_of(core * half + c * width, 128), width)
        out_ref[:, cols] = (f32(att_ref[:, cols]) + total).astype(jnp.bfloat16)

    reduce_a(0)
    reduce_a(1)
    reduce_b(0)
    reduce_a(2)
    reduce_b(1)
    reduce_c(0)
    reduce_a(3)
    reduce_b(2)
    reduce_c(1)
    reduce_d(0)
    reduce_b(3)
    reduce_c(2)
    reduce_d(1)
    combine(0)
    reduce_c(3)
    reduce_d(2)
    combine(1)
    reduce_d(3)
    combine(2)
    combine(3)

    last = remote(contrib_sib, contrib, pre_s.at[3], pre_r.at[3], sib)
    last.start()
    last.wait_recv()
    cols = pl.ds(pl.multiple_of((1 - core) * half, 128), half)
    out_ref[:, cols] = (f32(att_ref[:, cols]) + contrib[...]).astype(jnp.bfloat16)

    started = [send_meta, send_nrm, send_down, last] + sent_hidden
    for c in range(NC):
        started += dispatches[c] + gather[c] + shares[c] + reduce[c] + returns[c]
    for copy in started:
        copy.wait_send()


def experts(attended, norm_gain, expert_ids, expert_weights, gate_weight, up_weight, down_weight):
    d = attended.shape[1]
    half = d // 2
    width = half // NC
    bf, f32 = jnp.bfloat16, jnp.float32
    meta = jnp.pad(
        jnp.concatenate([expert_ids.T.astype(f32), expert_weights.T], axis=0), ((0, 4), (0, 112))
    )
    vmem = pl.BlockSpec(memory_space=pltpu.VMEM)
    anyspace = pl.BlockSpec(memory_space=pl.ANY)
    dma = pltpu.SemaphoreType.DMA
    block = (8, 16, width)
    return pl.pallas_call(
        experts_kernel,
        out_shape=jax.ShapeDtypeStruct(attended.shape, bf),
        in_specs=[vmem, vmem, vmem, anyspace, anyspace, anyspace],
        out_specs=vmem,
        scratch_shapes=[
            pltpu.VMEM((d, 768), bf),
            pltpu.VMEM((768, half), bf),
            pltpu.VMEM((8, 128), f32),
            pltpu.VMEM((2, 16, half), bf),
            pltpu.VMEM((16, half), bf),
            pltpu.VMEM((NC,) + block, bf),
            pltpu.VMEM((NC, 8) + block, bf),
            pltpu.VMEM((NC, 8) + block, bf),
            pltpu.VMEM((4, 256, 768), f32),
            pltpu.VMEM((4, 256, 768), bf),
            pltpu.VMEM((NC, 8) + block, bf),
            pltpu.VMEM((NC, 2) + block, bf),
            pltpu.VMEM((NC,) + block, bf),
            pltpu.VMEM((NC,) + block, bf),
            pltpu.VMEM((NC, 2, 4, 16, width), bf),
            pltpu.VMEM((NC, 2) + block, bf),
            pltpu.VMEM((NC,) + block, bf),
            pltpu.VMEM((NC,) + block, bf),
            pltpu.VMEM((16, half), f32),
            pltpu.VMEM((16, half), f32),
            dma((3,)),
            dma((4,)),
            dma((4,)),
            dma((NC, 7)),
            dma((NC, 7)),
            dma((NC, 8)),
            dma((NC, 8)),
            dma((NC, 8)),
            dma((NC, 8)),
            dma((4,)),
            dma((4,)),
            dma((NC, 8)),
            dma((NC, 8)),
            dma((NC, 7)),
            dma((NC, 7)),
        ],
        compiler_params=pltpu.CompilerParams(
            collective_id=1, has_side_effects=True, vmem_limit_bytes=VMEM_LIMIT
        ),
        cost_estimate=pl.CostEstimate(
            flops=2 * 3 * 1024 * d * 384, bytes_accessed=3 * d * 384 * 2, transcendentals=1024 * 384
        ),
        name="experts",
    )(attended, norm_gain.reshape(1, d), meta, gate_weight, up_weight, down_weight)


def row_positions(block_order, start, count, half):
    rows = start + jnp.arange(count, dtype=jnp.int32)
    blocks = rows // half
    table = (blocks[:, None] == jnp.arange(block_order.shape[0], dtype=jnp.int32)[None, :]).astype(
        jnp.int32
    )
    first = jnp.sum(table * block_order[None, :], axis=1)
    return first * half + rows % half


def on_device(
    stream,
    queries,
    key_head_rows,
    value_head_rows,
    block_order,
    out_weight,
    norm_gain,
    gate_weight,
    up_weight,
    down_weight,
    expert_ids,
    expert_weights,
):
    n_exp = lax.axis_size("exp")
    block_rows = queries.shape[0]
    half = block_rows // 2
    heads = queries.shape[1] // PER_LANE_DIM
    kv_heads = key_head_rows.shape[1] // PER_LANE_DIM
    head_group = heads // kv_heads
    query_pos = row_positions(block_order, lax.axis_index("ctx") * block_rows, block_rows, half)
    heads_of_query = queries.reshape(block_rows, kv_heads, head_group, PER_LANE_DIM)
    running_max = jnp.full((kv_heads, head_group, block_rows), -1e30, jnp.float32)
    key_piece = lax.all_gather(key_head_rows, "ctx", axis=0, tiled=True)
    value_piece = lax.all_gather(value_head_rows, "ctx", axis=0, tiled=True)
    count = key_piece.shape[0]
    key_pos = row_positions(block_order, jnp.int32(0), count, half)
    heads_of_key = key_piece.reshape(count, kv_heads, PER_LANE_DIM)
    heads_of_value = value_piece.reshape(count, kv_heads, PER_LANE_DIM)
    similarity_logits = jnp.einsum(
        "rkgd,tkd->kgrt", heads_of_query, heads_of_key, preferred_element_type=jnp.float32
    ) * PER_LANE_DIM ** (-0.5)
    visible = key_pos[None, :] <= query_pos[:, None]
    similarity_logits = jnp.where(visible, similarity_logits, -1e30)
    new_max = jnp.maximum(running_max, jnp.max(similarity_logits, axis=-1))
    expd = jnp.where(visible, jnp.exp(similarity_logits - new_max[..., None]), 0.0)
    total = jnp.sum(expd, axis=-1)
    product = jnp.einsum(
        "kgrt,tkd->kgrd",
        expd.astype(jnp.bfloat16),
        heads_of_value,
        preferred_element_type=jnp.float32,
    )
    weighted = product
    running_max, total, weighted = (new_max, total, weighted)
    heads_out = (
        (weighted / total[..., None])
        .transpose(2, 0, 1, 3)
        .reshape(block_rows, heads * PER_LANE_DIM)
        .astype(jnp.bfloat16)
    )
    partial_proj = jnp.dot(
        heads_out,
        lax.all_gather(out_weight, "ctx", axis=1, tiled=True),
        preferred_element_type=jnp.float32,
    )
    moe_rows = stream.shape[0]
    summed_output = lax.psum_scatter(
        partial_proj.astype(jnp.bfloat16), "exp", scatter_dimension=0, tiled=True
    ).astype(jnp.float32)
    attended = (stream.astype(jnp.float32) + summed_output).astype(jnp.bfloat16)
    mixed = experts(
        attended, norm_gain, expert_ids, expert_weights, gate_weight, up_weight, down_weight
    )
    return (attended, mixed)


def solution(mesh):
    in_specs = (
        P(("ctx", "exp"), None),
        P("ctx", "exp"),
        P("ctx", "exp"),
        P("ctx", "exp"),
        P(),
        P("exp", "ctx"),
        P(),
        P("exp", None, "ctx"),
        P("exp", None, "ctx"),
        P("exp", "ctx", None),
        P(("ctx", "exp"), None),
        P(("ctx", "exp"), None),
    )
    out_specs = (P(("ctx", "exp"), None), P(("ctx", "exp"), None))
    return jax.shard_map(
        on_device, mesh=mesh, in_specs=in_specs, out_specs=out_specs, check_vma=False
    )
```

```python
import functools

import jax
import jax.numpy as jnp
from jax import lax
from jax.experimental import pallas as pl
from jax.experimental.pallas import tpu as pltpu
from jax.sharding import PartitionSpec as P

PER_LANE_DIM = 128
MESH = pl.DeviceIdType.MESH
VMEM_LIMIT = 60 * 2**20
NC = 4


def place():
    ctx = lax.axis_index("ctx")
    exp = lax.axis_index("exp")
    return ctx // 4, lax.rem(ctx // 2, 2), lax.rem(ctx, 2), exp


def remote(src, dst, send, recv, device):
    return pltpu.make_async_remote_copy(
        src_ref=src, dst_ref=dst, send_sem=send, recv_sem=recv, device_id=device, device_id_type=MESH
    )


def greet(devices):
    barrier = pltpu.get_barrier_semaphore()
    for device in devices:
        pl.semaphore_signal(barrier, inc=1, device_id=device, device_id_type=MESH)
    pl.semaphore_wait(barrier, len(devices))


def slot_match(meta, core):
    row = lax.broadcasted_iota(jnp.int32, (128, 128), 0)
    lane = lax.broadcasted_iota(jnp.int32, (128, 128), 1)
    expert = (row // 16).astype(jnp.float32)
    first = (meta[0:1, :] == expert) & (lane < 16)
    second = (meta[1:2, :] == expert) & (lane < 16)
    named = jnp.where(first | second, 1.0, 0.0)
    earlier = jnp.where(row < lane, 1.0, 0.0)
    rank = jnp.dot(
        named.astype(jnp.bfloat16), earlier.astype(jnp.bfloat16), preferred_element_type=jnp.float32
    )
    slot = lax.rem(row, 8).astype(jnp.float32)
    mine = lax.rem(row // 8, 2) == core
    match = jnp.where((rank == slot) & mine, named, 0.0)
    weight = match * jnp.where(first, meta[2:3, :], meta[3:4, :])
    return match[:, :16].astype(jnp.bfloat16), weight.T[:16, :]


def experts_kernel(
    att_ref, gain_ref, meta_ref, gate_ref, up_ref, down_ref, out_ref,
    wgu, wd, meta_sib, nrm, nsib, disp, rows, rows_sib, acc, hid, part,
    got1, got2, got3, got4, got5, final, back, contrib, contrib_sib,
    load_sem, pre_s, pre_r, disp_s, disp_r, ga_s, ga_r, sib_s, sib_r, hid_s, hid_r, rs_s, rs_r, back_s, back_r,
):
    z, xh, core, exp = place()
    width = rows.shape[-1]
    half = NC * width
    up_z, down_z, far_z = lax.rem(z + 1, 4), lax.rem(z + 3, 4), lax.rem(z + 2, 4)

    def dev(a, b, c=None, e=None):
        return (a * 4 + b * 2 + (core if c is None else c), exp if e is None else e)

    def blk(a, b):
        return a * 2 + b

    zp, zm, xp, sib = dev(up_z, xh), dev(down_z, xh), dev(z, 1 - xh), dev(z, xh, 1 - core)
    peers = [lax.rem(exp + j, 8) for j in range(1, 8)]
    own_block = blk(z, xh)

    loads = [
        pltpu.make_async_copy(gate_ref.at[0], wgu.at[:, pl.ds(0, 384)], load_sem.at[0]),
        pltpu.make_async_copy(up_ref.at[0], wgu.at[:, pl.ds(384, 384)], load_sem.at[1]),
        pltpu.make_async_copy(
            down_ref.at[0, :, pl.ds(pl.multiple_of(core * half, 128), half)],
            wd.at[pl.ds(pl.multiple_of(core * 384, 128), 384)],
            load_sem.at[2],
        ),
    ]
    for load in loads:
        load.start()
    greet([zp, zm, xp, sib] + [dev(z, xh, None, e) for e in peers])

    send_meta = remote(meta_ref, meta_sib, pre_s.at[0], pre_r.at[0], sib)
    send_meta.start()
    wide = att_ref[...].astype(jnp.float32)
    normed = (
        wide * lax.rsqrt(jnp.mean(wide * wide, axis=-1, keepdims=True) + 1e-05) * gain_ref[...]
    ).astype(jnp.bfloat16)
    nrm[0] = normed[:, :half]
    nrm[1] = normed[:, half:]
    send_nrm = remote(nrm.at[1 - core], nsib, pre_s.at[1], pre_r.at[1], sib)
    send_nrm.start()
    match_own, weight_own = slot_match(meta_ref[...], core)
    send_meta.wait_recv()
    match_sib, weight_sib = slot_match(meta_sib[...], 1 - core)
    send_nrm.wait_recv()

    dispatches = []
    for c in range(NC):
        cols = pl.ds(c * width, width)
        picked = jnp.dot(match_own, nrm[core, :, cols], preferred_element_type=jnp.float32) + jnp.dot(
            match_sib, nsib[:, cols], preferred_element_type=jnp.float32
        )
        disp[c] = picked.astype(jnp.bfloat16).reshape(8, 16, width)
        sends = []
        for j, e in enumerate(peers):
            copy = remote(
                disp.at[c, e], rows.at[c, own_block, exp], disp_s.at[c, j], disp_r.at[c, j],
                dev(z, xh, None, e),
            )
            copy.start()
            sends.append(copy)
        rows[c, own_block, exp] = disp[c, exp]
        dispatches.append(sends)
    send_down = remote(
        down_ref.at[0, :, pl.ds(pl.multiple_of((1 - core) * half, 128), half)],
        wd.at[pl.ds(pl.multiple_of(core * 384, 128), 384)],
        pre_s.at[2], pre_r.at[2], sib,
    )
    send_down.start()

    gather = [[None] * 8 for _ in range(NC)]
    shares = [[] for _ in range(NC)]

    def forward(c, k, block, device, part_of=None):
        ref = rows.at[c, block] if part_of is None else rows.at[c, block, pl.ds(part_of * 4, 4)]
        gather[c][k] = remote(ref, ref, ga_s.at[c, k], ga_r.at[c, k], device)
        gather[c][k].start()

    def share(c, block):
        j = len(shares[c])
        copy = remote(rows.at[c, block], rows_sib.at[c, block], sib_s.at[c, j], sib_r.at[c, j], sib)
        copy.start()
        shares[c].append(copy)

    def gather_a(c):
        for copy in dispatches[c]:
            copy.wait_recv()
        forward(c, 0, own_block, zp)
        forward(c, 1, own_block, zm)
        forward(c, 2, own_block, xp)
        share(c, own_block)

    def gather_b(c):
        gather[c][0].wait_recv()
        forward(c, 3, blk(down_z, xh), zp, 0)
        share(c, blk(down_z, xh))
        gather[c][1].wait_recv()
        forward(c, 4, blk(up_z, xh), zm, 1)
        share(c, blk(up_z, xh))
        gather[c][2].wait_recv()
        forward(c, 5, blk(z, 1 - xh), zp)
        forward(c, 6, blk(z, 1 - xh), zm)
        share(c, blk(z, 1 - xh))

    def gather_c(c):
        gather[c][3].wait_recv()
        gather[c][4].wait_recv()
        forward(c, 7, blk(far_z, xh), xp)
        share(c, blk(far_z, xh))

    def gather_d(c):
        gather[c][5].wait_recv()
        share(c, blk(down_z, 1 - xh))
        gather[c][6].wait_recv()
        share(c, blk(up_z, 1 - xh))
        gather[c][7].wait_recv()
        share(c, blk(far_z, 1 - xh))

    def multiply(source, c, first_col, fresh):
        base = pl.multiple_of(first_col + c * width, 128)

        def body(i, carry):
            lhs = source[c, pl.ds(i * 2, 2)].reshape(256, width)
            term = jnp.dot(lhs, wgu[pl.ds(base, width), :], preferred_element_type=jnp.float32)
            if fresh:
                acc[i] = term
            else:
                acc[i] += term
            return carry

        lax.fori_loop(0, 4, body, 0)

    def multiply_own(c):
        if c == 0:
            loads[0].wait()
            loads[1].wait()
        multiply(rows, c, core * half, c == 0)

    def multiply_sib(c):
        for copy in shares[c]:
            copy.wait_recv()
        multiply(rows_sib, c, (1 - core) * half, False)

    gather_a(0)
    gather_a(1)
    gather_b(0)
    gather_c(0)
    gather_a(2)
    gather_b(1)
    gather_d(0)
    multiply_own(0)
    gather_c(1)
    gather_a(3)
    gather_b(2)
    gather_d(1)
    multiply_sib(0)
    gather_c(2)
    multiply_own(1)
    gather_b(3)
    gather_d(2)
    multiply_sib(1)
    gather_c(3)
    multiply_own(2)
    multiply_sib(2)
    gather_d(3)
    multiply_own(3)
    multiply_sib(3)

    mine = pl.ds(pl.multiple_of(core * 384, 128), 384)
    sent_hidden = []
    for i in range(4):
        gate_part = acc[i, :, :384]
        up_part = acc[i, :, 384:]
        hid[i, :, mine] = (gate_part / (1.0 + jnp.exp(-gate_part)) * up_part).astype(jnp.bfloat16)
        copy = remote(hid.at[i, :, mine], hid.at[i, :, mine], hid_s.at[i], hid_r.at[i], sib)
        copy.start()
        sent_hidden.append(copy)
    loads[2].wait()
    send_down.wait_recv()
    for copy in sent_hidden:
        copy.wait_recv()

    reduce = [[None] * 8 for _ in range(NC)]
    returns = []

    def send_sum(c, k, src, dst, device):
        reduce[c][k] = remote(src, dst, rs_s.at[c, k], rs_r.at[c, k], device)
        reduce[c][k].start()

    def f32(value):
        return value.astype(jnp.float32)

    def reduce_a(c):
        def body(i, carry):
            out = jnp.dot(hid[i], wd[:, c * width : (c + 1) * width], preferred_element_type=jnp.float32)
            part[c, pl.ds(i * 2, 2)] = out.astype(jnp.bfloat16).reshape(2, 8, 16, width)
            return carry

        lax.fori_loop(0, 4, body, 0)
        send_sum(c, 0, part.at[c, blk(up_z, 1 - xh)], got1.at[c, 0], zp)
        send_sum(c, 1, part.at[c, blk(down_z, 1 - xh)], got1.at[c, 1], zm)
        send_sum(c, 2, part.at[c, blk(far_z, 1 - xh)], got2.at[c], xp)

    def reduce_b(c):
        reduce[c][2].wait_recv()
        block = blk(far_z, xh)
        part[c, block] = (f32(part[c, block]) + f32(got2[c])).astype(jnp.bfloat16)
        send_sum(c, 3, part.at[c, block, pl.ds(0, 4)], got4.at[c, 0], zm)
        send_sum(c, 4, part.at[c, block, pl.ds(4, 4)], got4.at[c, 1], zp)
        reduce[c][0].wait_recv()
        reduce[c][1].wait_recv()
        block = blk(z, 1 - xh)
        part[c, block] = (f32(part[c, block]) + f32(got1[c, 0]) + f32(got1[c, 1])).astype(jnp.bfloat16)
        send_sum(c, 5, part.at[c, block], got3.at[c], xp)

    def reduce_c(c):
        reduce[c][3].wait_recv()
        block = blk(down_z, xh)
        part[c, block, 0:4] = (f32(part[c, block, 0:4]) + f32(got4[c, 0])).astype(jnp.bfloat16)
        send_sum(c, 6, part.at[c, block], got5.at[c, 0], zm)
        reduce[c][4].wait_recv()
        block = blk(up_z, xh)
        part[c, block, 4:8] = (f32(part[c, block, 4:8]) + f32(got4[c, 1])).astype(jnp.bfloat16)
        send_sum(c, 7, part.at[c, block], got5.at[c, 1], zp)

    def reduce_d(c):
        reduce[c][5].wait_recv()
        reduce[c][6].wait_recv()
        reduce[c][7].wait_recv()
        final[c] = (
            f32(part[c, own_block]) + f32(got3[c]) + (f32(got5[c, 0]) + f32(got5[c, 1]))
        ).astype(jnp.bfloat16)
        sends = []
        for j, e in enumerate(peers):
            copy = remote(
                final.at[c, e], back.at[c, exp], back_s.at[c, j], back_r.at[c, j], dev(z, xh, None, e)
            )
            copy.start()
            sends.append(copy)
        back[c, exp] = final[c, exp]
        returns.append(sends)

    def combine(c):
        for copy in returns[c]:
            copy.wait_recv()
        values = f32(back[c].reshape(128, width))
        contrib_sib[:, c * width : (c + 1) * width] = jnp.dot(
            weight_sib, values, precision=lax.Precision.HIGHEST, preferred_element_type=jnp.float32
        )
        total = jnp.dot(
            weight_own, values, precision=lax.Precision.HIGHEST, preferred_element_type=jnp.float32
        )
        cols = pl.ds(pl.multiple_of(core * half + c * width, 128), width)
        out_ref[:, cols] = (f32(att_ref[:, cols]) + total).astype(jnp.bfloat16)

    reduce_a(0)
    reduce_a(1)
    reduce_b(0)
    reduce_a(2)
    reduce_b(1)
    reduce_c(0)
    reduce_a(3)
    reduce_b(2)
    reduce_c(1)
    reduce_d(0)
    reduce_b(3)
    reduce_c(2)
    reduce_d(1)
    combine(0)
    reduce_c(3)
    reduce_d(2)
    combine(1)
    reduce_d(3)
    combine(2)
    combine(3)

    last = remote(contrib_sib, contrib, pre_s.at[3], pre_r.at[3], sib)
    last.start()
    last.wait_recv()
    cols = pl.ds(pl.multiple_of((1 - core) * half, 128), half)
    out_ref[:, cols] = (f32(att_ref[:, cols]) + contrib[...]).astype(jnp.bfloat16)

    started = [send_meta, send_nrm, send_down, last] + sent_hidden
    for c in range(NC):
        started += dispatches[c] + gather[c] + shares[c] + reduce[c] + returns[c]
    for copy in started:
        copy.wait_send()


def experts(attended, norm_gain, expert_ids, expert_weights, gate_weight, up_weight, down_weight):
    d = attended.shape[1]
    half = d // 2
    width = half // NC
    bf, f32 = jnp.bfloat16, jnp.float32
    meta = jnp.pad(
        jnp.concatenate([expert_ids.T.astype(f32), expert_weights.T], axis=0), ((0, 4), (0, 112))
    )
    vmem = pl.BlockSpec(memory_space=pltpu.VMEM)
    anyspace = pl.BlockSpec(memory_space=pl.ANY)
    dma = pltpu.SemaphoreType.DMA
    block = (8, 16, width)
    return pl.pallas_call(
        experts_kernel,
        out_shape=jax.ShapeDtypeStruct(attended.shape, bf),
        in_specs=[vmem, vmem, vmem, anyspace, anyspace, anyspace],
        out_specs=vmem,
        scratch_shapes=[
            pltpu.VMEM((d, 768), bf),
            pltpu.VMEM((768, half), bf),
            pltpu.VMEM((8, 128), f32),
            pltpu.VMEM((2, 16, half), bf),
            pltpu.VMEM((16, half), bf),
            pltpu.VMEM((NC,) + block, bf),
            pltpu.VMEM((NC, 8) + block, bf),
            pltpu.VMEM((NC, 8) + block, bf),
            pltpu.VMEM((4, 256, 768), f32),
            pltpu.VMEM((4, 256, 768), bf),
            pltpu.VMEM((NC, 8) + block, bf),
            pltpu.VMEM((NC, 2) + block, bf),
            pltpu.VMEM((NC,) + block, bf),
            pltpu.VMEM((NC,) + block, bf),
            pltpu.VMEM((NC, 2, 4, 16, width), bf),
            pltpu.VMEM((NC, 2) + block, bf),
            pltpu.VMEM((NC,) + block, bf),
            pltpu.VMEM((NC,) + block, bf),
            pltpu.VMEM((16, half), f32),
            pltpu.VMEM((16, half), f32),
            dma((3,)),
            dma((4,)),
            dma((4,)),
            dma((NC, 7)),
            dma((NC, 7)),
            dma((NC, 8)),
            dma((NC, 8)),
            dma((NC, 8)),
            dma((NC, 8)),
            dma((4,)),
            dma((4,)),
            dma((NC, 8)),
            dma((NC, 8)),
            dma((NC, 7)),
            dma((NC, 7)),
        ],
        compiler_params=pltpu.CompilerParams(
            collective_id=1, has_side_effects=True, vmem_limit_bytes=VMEM_LIMIT
        ),
        cost_estimate=pl.CostEstimate(
            flops=2 * 3 * 1024 * d * 384, bytes_accessed=3 * d * 384 * 2, transcendentals=1024 * 384
        ),
        name="experts",
    )(attended, norm_gain.reshape(1, d), meta, gate_weight, up_weight, down_weight)


def attention_kernel(
    q_ref, k_ref, v_ref, qpos_ref, kpos_ref, weight_ref, stream_ref, out_ref,
    kv, bias, wcat, heads, part, got, summed, blocks,
    kv_s, kv_r, kvs_s, kvs_r, w_load, w_s, w_r, h_s, h_r, p_s, p_r, c_s, c_r,
):
    z, xh, core, exp = place()
    up_z, down_z, far_z = lax.rem(z + 1, 4), lax.rem(z + 3, 4), lax.rem(z + 2, 4)

    def dev(a, b, c=None, e=None):
        return (a * 4 + b * 2 + (core if c is None else c), exp if e is None else e)

    def ctx_of(a, b, c):
        return a * 4 + b * 2 + c

    zp, zm, xp, sib = dev(up_z, xh), dev(down_z, xh), dev(z, 1 - xh), dev(z, xh, 1 - core)
    turns = [(dz, dx) for dx in (0, 1) for dz in (1, 3, 2, 0) if (dz, dx) != (0, 0)]
    chips = [(lax.rem(z + dz, 4), lax.rem(xh + dx, 2)) for dz, dx in turns]
    sources = [(lax.rem(z + 4 - dz, 4), lax.rem(xh + dx, 2)) for dz, dx in turns]
    peers = [lax.rem(exp + j, 8) for j in range(1, 8)]
    me = ctx_of(z, xh, core)

    own_cols = pl.ds(pl.multiple_of((xh * 2 + core) * 384, 128), 384)
    load = pltpu.make_async_copy(weight_ref, wcat.at[:, own_cols], w_load.at[0])
    load.start()
    kv[0, me] = k_ref[...]
    kv[1, me] = v_ref[...]
    greet([dev(a, b) for a, b in chips] + [sib] + [dev(z, xh, None, e) for e in peers])

    started = []

    def send(src, dst, s, r, device):
        copy = remote(src, dst, s, r, device)
        copy.start()
        started.append(copy)
        return copy

    gathers = [
        send(kv.at[:, me], kv.at[:, me], kv_s.at[j], kv_r.at[j], dev(a, b))
        for j, (a, b) in enumerate(chips)
    ]
    shares = [send(kv.at[:, me], kv.at[:, me], kvs_s.at[7], kvs_r.at[7], sib)]
    w_x = send(weight_ref, wcat.at[:, own_cols], w_s.at[0], w_r.at[0], xp)
    w_sib = send(weight_ref, wcat.at[:, own_cols], w_s.at[1], w_r.at[1], sib)
    bias[...] = jnp.where(kpos_ref[...] <= qpos_ref[...], 0.0, -1e30)
    for j, (a, b) in enumerate(sources):
        gathers[j].wait_recv()
        slot = kv.at[:, ctx_of(a, b, core)]
        shares.append(send(slot, slot, kvs_s.at[j], kvs_r.at[j], sib))
    for copy in shares:
        copy.wait_recv()

    scale = PER_LANE_DIM ** (-0.5) * 1.4426950408889634

    def attend(half):
        def body(i, carry):
            first = pl.multiple_of(half * 512 + i * 256, 128)
            pair = q_ref[:, pl.ds(first, 256)]
            q = jnp.concatenate([pair[:, :128], pair[:, 128:]], axis=0)
            keys = kv[0].reshape(2048, 128)
            values = kv[1].reshape(2048, 128)
            logits = lax.dot_general(
                q, keys, (((1,), (1,)), ((), ())), preferred_element_type=jnp.float32
            )
            logits = logits.reshape(2, 128, 2048) * scale + bias[...][None]
            peak = jnp.max(logits, axis=-1, keepdims=True)
            expd = jnp.exp2(logits - peak)
            total = jnp.sum(expd, axis=-1, keepdims=True)
            weighted = jnp.dot(
                expd.astype(jnp.bfloat16).reshape(256, 2048), values, preferred_element_type=jnp.float32
            )
            result = (weighted.reshape(2, 128, 128) / total).astype(jnp.bfloat16)
            out = jnp.concatenate([result[0], result[1]], axis=1)
            heads[z, half, :, pl.ds(pl.multiple_of(i * 256, 128), 256)] = out
            return carry

        lax.fori_loop(0, 2, body, 0)

    def send_heads(k, a, half, device):
        return send(heads.at[a, half], heads.at[a, half], h_s.at[k], h_r.at[k], device)

    attend(0)
    moves = [send_heads(0, z, 0, zp), send_heads(1, z, 0, zm)]
    attend(1)
    moves += [send_heads(2, z, 1, zp), send_heads(3, z, 1, zm)]
    w_x.wait_recv()
    other_cols = pl.ds(pl.multiple_of(((1 - xh) * 2 + core) * 384, 128), 384)
    w_far = send(wcat.at[:, other_cols], wcat.at[:, other_cols], w_s.at[2], w_r.at[2], sib)
    load.wait()
    w_sib.wait_recv()
    w_far.wait_recv()

    def project(t, a):
        product = jnp.dot(heads[a, 0], wcat[:512, :], preferred_element_type=jnp.float32)
        product += jnp.dot(heads[a, 1], wcat[512:, :], preferred_element_type=jnp.float32)
        part[a] = product.astype(jnp.bfloat16).reshape(8, 16, 1536)
        copies = [
            send(part.at[a, e], got.at[a, exp], p_s.at[t, j], p_r.at[t, j], dev(z, xh, None, e))
            for j, e in enumerate(peers)
        ]
        got[a, exp] = part[a, exp]
        return copies

    def add_up(t, a, copies):
        for copy in copies:
            copy.wait_recv()
        total = jnp.sum(got[a].astype(jnp.float32), axis=0).astype(jnp.bfloat16)
        if t == 0:
            blocks[z] = total
            return None
        summed[a] = total
        return send(summed.at[a], blocks.at[z], c_s.at[t - 1], c_r.at[t - 1], dev(a, xh))

    sums = [project(0, z)]
    moves[0].wait_recv()
    moves.append(send_heads(4, down_z, 0, zp))
    moves[1].wait_recv()
    moves[2].wait_recv()
    moves[3].wait_recv()
    moves.append(send_heads(5, up_z, 1, zm))
    sums.append(project(1, down_z))
    sums.append(project(2, up_z))
    moves[4].wait_recv()
    moves[5].wait_recv()
    sums.append(project(3, far_z))
    last = [add_up(t, a, sums[t]) for t, a in enumerate((z, down_z, up_z, far_z))]
    for copy in last[1:]:
        copy.wait_recv()
    for a in range(4):
        cols = slice(a * 1536, (a + 1) * 1536)
        out_ref[:, cols] = (
            stream_ref[:, cols].astype(jnp.float32) + blocks[a].astype(jnp.float32)
        ).astype(jnp.bfloat16)
    for copy in started:
        copy.wait_send()


def attention(stream, queries, keys, values, block_order, out_weight):
    bf, f32 = jnp.bfloat16, jnp.float32
    rows = queries.shape[0]
    kpos = (block_order[:, None] * 64 + jnp.arange(64, dtype=jnp.int32)[None, :]).reshape(1, 2048)
    qpos = lax.dynamic_slice_in_dim(kpos, lax.axis_index("ctx") * rows, rows, 1).reshape(rows, 1)
    vmem = pl.BlockSpec(memory_space=pltpu.VMEM)
    dma = pltpu.SemaphoreType.DMA
    return pl.pallas_call(
        attention_kernel,
        out_shape=jax.ShapeDtypeStruct(stream.shape, bf),
        in_specs=[vmem] * 5 + [pl.BlockSpec(memory_space=pl.ANY), vmem],
        out_specs=vmem,
        scratch_shapes=[
            pltpu.VMEM((2, 16, 128, 128), bf),
            pltpu.VMEM((128, 2048), f32),
            pltpu.VMEM((1024, 1536), bf),
            pltpu.VMEM((4, 2, 128, 512), bf),
            pltpu.VMEM((4, 8, 16, 1536), bf),
            pltpu.VMEM((4, 8, 16, 1536), bf),
            pltpu.VMEM((4, 16, 1536), bf),
            pltpu.VMEM((4, 16, 1536), bf),
            dma((7,)),
            dma((7,)),
            dma((8,)),
            dma((8,)),
            dma((1,)),
            dma((3,)),
            dma((3,)),
            dma((6,)),
            dma((6,)),
            dma((4, 7)),
            dma((4, 7)),
            dma((3,)),
            dma((3,)),
        ],
        compiler_params=pltpu.CompilerParams(
            collective_id=0, has_side_effects=True, vmem_limit_bytes=VMEM_LIMIT
        ),
        cost_estimate=pl.CostEstimate(
            flops=2 * 1024 * 128 * 2048 * 2 + 2 * 512 * 1024 * 1536,
            bytes_accessed=1024 * 384 * 2,
            transcendentals=1024 * 2048,
        ),
        name="attention",
    )(queries, keys, values, qpos, kpos, out_weight, stream)


def on_device(
    stream,
    queries,
    key_head_rows,
    value_head_rows,
    block_order,
    out_weight,
    norm_gain,
    gate_weight,
    up_weight,
    down_weight,
    expert_ids,
    expert_weights,
):
    attended = attention(stream, queries, key_head_rows, value_head_rows, block_order, out_weight)
    mixed = experts(
        attended, norm_gain, expert_ids, expert_weights, gate_weight, up_weight, down_weight
    )
    return (attended, mixed)


def solution(mesh):
    in_specs = (
        P(("ctx", "exp"), None),
        P("ctx", "exp"),
        P("ctx", "exp"),
        P("ctx", "exp"),
        P(),
        P("exp", "ctx"),
        P(),
        P("exp", None, "ctx"),
        P("exp", None, "ctx"),
        P("exp", "ctx", None),
        P(("ctx", "exp"), None),
        P(("ctx", "exp"), None),
    )
    out_specs = (P(("ctx", "exp"), None), P(("ctx", "exp"), None))
    return jax.shard_map(
        on_device, mesh=mesh, in_specs=in_specs, out_specs=out_specs, check_vma=False
    )
```

```python
import jax
import jax.numpy as jnp
from jax import lax
from jax.experimental import pallas as pl
from jax.experimental.pallas import tpu as pltpu
from jax.sharding import PartitionSpec as P

HEAD = 128
MESH = pl.DeviceIdType.MESH
VMEM_LIMIT = 62 * 2**20
WIDTHS = (384, 768, 768, 768, 384)
NC = len(WIDTHS)
STARTS = tuple(sum(WIDTHS[:c]) for c in range(NC))
BF16, F32 = jnp.bfloat16, jnp.float32


def f32(value):
    return value.astype(F32)


def dot(a, b):
    return jnp.dot(a, b, preferred_element_type=F32)


def remote(src, dst, send, recv, device):
    return pltpu.make_async_remote_copy(
        src_ref=src, dst_ref=dst, send_sem=send, recv_sem=recv, device_id=device, device_id_type=MESH
    )


def greet(devices):
    barrier = pltpu.get_barrier_semaphore()
    for device in devices:
        pl.semaphore_signal(barrier, inc=1, device_id=device, device_id_type=MESH)
    pl.semaphore_wait(barrier, len(devices))


def slot_match(meta, core):
    row = lax.broadcasted_iota(jnp.int32, (128, 128), 0)
    lane = lax.broadcasted_iota(jnp.int32, (128, 128), 1)
    expert = f32(row // 16)
    first = (meta[0:1, :] == expert) & (lane < 16)
    second = (meta[1:2, :] == expert) & (lane < 16)
    named = jnp.where(first | second, 1.0, 0.0)
    earlier = jnp.where(row < lane, 1.0, 0.0)
    rank = dot(named.astype(BF16), earlier.astype(BF16))
    slot = f32(lax.rem(row, 8))
    mine = lax.rem(row // 8, 2) == core
    match = jnp.where((rank == slot) & mine, named, 0.0)
    weight = match * jnp.where(first, meta[2:3, :], meta[3:4, :])
    return match[:, :16].astype(BF16), weight.T[:16, :]


def staged(count, *stages):
    for step in range(count + max(late for late, _ in stages)):
        for late, stage in stages:
            if 0 <= step - late < count:
                stage(step - late)


def layer_kernel(
    q_ref, k_ref, v_ref, order_ref, proj_ref, stream_ref, gain_ref, ids_ref, mix_ref,
    gate_ref, up_ref, down_ref, att_ref, out_ref,
    kv, kpos, bias, wcat, heads, proj, got_y, sums, half_sum, got_x, summed, blocks,
    wgu, wd, meta, meta_sib, nrm, nsib, disp, rows, rows_sib, acc, hid, part,
    got1, got2, got3, got4, got5, final, back, contrib, contrib_sib,
    load_sem, pre_s, pre_r, kv_s, kv_r, w_s, w_r, h_s, h_r, y_s, y_r, x_s, x_r, b_s, b_r,
    disp_s, disp_r, ga_s, ga_r, sib_s, sib_r, hid_s, hid_r, rs_s, rs_r, back_s, back_r,
):
    ctx = lax.axis_index("ctx")
    exp = lax.axis_index("exp")
    z, xh, core = ctx // 4, lax.rem(ctx // 2, 2), lax.rem(ctx, 2)
    y, xl = exp // 2, lax.rem(exp, 2)
    up_z, down_z, far_z = lax.rem(z + 1, 4), lax.rem(z + 3, 4), lax.rem(z + 2, 4)
    half = sum(WIDTHS)

    def dev(a, b, c=None, e=None):
        return (a * 4 + b * 2 + (core if c is None else c), exp if e is None else e)

    def blk(a, b):
        return a * 2 + b

    zp, zm, xp, sib = dev(up_z, xh), dev(down_z, xh), dev(z, 1 - xh), dev(z, xh, 1 - core)
    peers = [lax.rem(exp + j, 8) for j in range(1, 8)]
    columns = [lax.rem(y + j, 4) for j in range(1, 4)]
    own = blk(z, xh)
    far = dev(far_z, xh)
    started = []

    def send(src, dst, s, r, device):
        copy = remote(src, dst, s, r, device)
        copy.start()
        started.append(copy)
        return copy

    def spread(view, s, r):
        copies = [None] * 8

        def forward(k, block, device, piece=None):
            ref = view(block, piece)
            copies[k] = send(ref, ref, s.at[k], r.at[k], device)

        def first():
            forward(0, own, zp)
            forward(1, own, zm)
            forward(2, own, xp)

        def second():
            copies[0].wait_recv()
            forward(3, blk(down_z, xh), zp, 0)
            copies[1].wait_recv()
            forward(4, blk(up_z, xh), zm, 1)
            copies[2].wait_recv()
            forward(5, blk(z, 1 - xh), zp)
            forward(6, blk(z, 1 - xh), zm)

        def third():
            copies[3].wait_recv()
            copies[4].wait_recv()
            forward(7, blk(far_z, xh), xp)

        def fourth():
            copies[5].wait_recv()
            copies[6].wait_recv()
            copies[7].wait_recv()

        return first, second, third, fourth

    def proj_cols(a, b):
        return pl.ds(pl.multiple_of((a * 2 + b) * 384, 128), 384)

    own_cols = proj_cols(xh, core)
    core_cols = pl.ds(pl.multiple_of(core * 384, 128), 384)
    core_half = pl.ds(pl.multiple_of(core * half, 128), half)
    sib_half = pl.ds(pl.multiple_of((1 - core) * half, 128), half)
    loads = [
        pltpu.make_async_copy(proj_ref, wcat.at[:, own_cols], load_sem.at[0]),
        pltpu.make_async_copy(gate_ref.at[0], wgu.at[:, pl.ds(0, 384)], load_sem.at[1]),
        pltpu.make_async_copy(up_ref.at[0], wgu.at[:, pl.ds(384, 384)], load_sem.at[2]),
        pltpu.make_async_copy(down_ref.at[0, :, core_half], wd.at[core_cols], load_sem.at[3]),
    ]
    for load in loads:
        load.start()
    kv[core, xh, z, 0] = k_ref[...]
    kv[core, xh, z, 1] = v_ref[...]
    meta[...] = jnp.zeros_like(meta)
    meta[0:2, 0:16] = f32(ids_ref[...])
    meta[2:4, 0:16] = mix_ref[...]
    greet([zp, zm, far, xp, sib] + [dev(z, xh, None, e) for e in peers])

    def send_kv(k, a, b, device):
        return send(kv.at[core, a, b], kv.at[core, a, b], kv_s.at[k], kv_r.at[k], device)

    from_x = send_kv(0, xh, z, xp)
    column = [send_kv(1 + j, xh, z, device) for j, device in enumerate((zp, zm, far))]
    piece = 256
    send_w = [
        send(
            proj_ref.at[pl.ds(i * piece, piece)], wcat.at[pl.ds(i * piece, piece), own_cols],
            w_s.at[i], w_r.at[i], xp,
        )
        for i in range(4)
    ]
    send_w_sib = send(proj_ref, wcat.at[:, own_cols], pre_s.at[0], pre_r.at[0], sib)
    send_meta = send(meta, meta_sib, pre_s.at[1], pre_r.at[1], sib)
    from_x.wait_recv()
    column += [send_kv(4 + j, 1 - xh, z, device) for j, device in enumerate((zp, zm, far))]
    lane = lax.broadcasted_iota(jnp.int32, (1, 128), 1)
    for slot in range(16):
        place = slot % 4 * 4 + slot // 4 % 2 * 2 + slot // 8
        first = jnp.where(lane < 64, order_ref[2 * place], order_ref[2 * place + 1])
        kpos[:, slot * 128 : (slot + 1) * 128] = first * 64 + lax.rem(lane, 64)
    row = lax.broadcasted_iota(jnp.int32, (128, 1), 0)
    qpos = jnp.where(row < 64, order_ref[2 * ctx], order_ref[2 * ctx + 1]) * 64 + lax.rem(row, 64)
    bias[...] = jnp.where(kpos[...] <= qpos, 0.0, -1e30)
    match_own, weight_own = slot_match(meta[...], core)
    for copy in column[:3]:
        copy.wait_recv()
    share_kv = [send(kv.at[core, xh], kv.at[core, xh], kv_s.at[7], kv_r.at[7], sib)]
    send_meta.wait_recv()
    match_sib, weight_sib = slot_match(meta_sib[...], 1 - core)
    for copy in column[3:]:
        copy.wait_recv()
    share_kv.append(send(kv.at[core, 1 - xh], kv.at[core, 1 - xh], kv_s.at[8], kv_r.at[8], sib))
    for copy in share_kv:
        copy.wait_recv()

    scale = HEAD ** (-0.5) * 1.4426950408889634

    def attend(part_of):
        def body(i, carry):
            pair = q_ref[:, pl.ds(pl.multiple_of(part_of * 512 + i * 256, 128), 256)]
            q = jnp.concatenate([pair[:, :128], pair[:, 128:]], axis=0)
            keys = kv[:, :, :, 0].reshape(2048, HEAD)
            values = kv[:, :, :, 1].reshape(2048, HEAD)
            logits = lax.dot_general(q, keys, (((1,), (1,)), ((), ())), preferred_element_type=F32)
            logits = logits.reshape(2, 128, 2048) * scale + bias[...][None]
            expd = jnp.exp2(logits - jnp.max(logits, axis=-1, keepdims=True))
            total = jnp.sum(expd, axis=-1, keepdims=True)
            weighted = dot(expd.astype(BF16).reshape(256, 2048), values)
            result = (weighted.reshape(2, 128, HEAD) / total).astype(BF16)
            heads[part_of, z, :, pl.ds(pl.multiple_of(i * 256, 128), 256)] = jnp.concatenate(
                [result[0], result[1]], axis=1
            )
            return carry

        lax.fori_loop(0, 2, body, 0)

    def send_heads(i, k, a, rows_of, device):
        view = heads.at[i, a, rows_of]
        return send(view, view, h_s.at[i, k], h_r.at[i, k], device)

    moves = []
    for i in range(2):
        attend(i)
        moves.append([send_heads(i, k, z, pl.ds(0, 128), device) for k, device in enumerate((zp, zm))])
    send_down = send(down_ref.at[0, :, sib_half], wd.at[core_cols], pre_s.at[2], pre_r.at[2], sib)
    far_w = []
    for i in range(4):
        send_w[i].wait_recv()
        view = wcat.at[pl.ds(i * piece, piece), proj_cols(1 - xh, core)]
        far_w.append(send(view, view, w_s.at[4 + i], w_r.at[4 + i], sib))
    for i in range(2):
        moves[i][0].wait_recv()
        moves[i].append(send_heads(i, 2, down_z, pl.ds(0, 64), zp))
        moves[i][1].wait_recv()
        moves[i].append(send_heads(i, 3, up_z, pl.ds(64, 64), zm))
    loads[0].wait()
    send_w_sib.wait_recv()
    for copy in far_w:
        copy.wait_recv()

    order = [z, down_z, up_z, far_z]
    to_y = [None] * 4
    to_x = [None] * 4
    to_block = [None] * 4

    def project(*turns):
        places = [order[t] for t in turns]
        product = 0.0
        for i in range(2):
            lhs = jnp.concatenate([heads[i, b] for b in places], axis=0)
            product += dot(lhs, wcat[i * 512 : (i + 1) * 512, :])
        for n, (t, b) in enumerate(zip(turns, places)):
            proj[b] = product[n * 128 : (n + 1) * 128].astype(BF16).reshape(4, 2, 16, 1536)
            to_y[t] = [
                send(proj.at[b, c], got_y.at[b, y], y_s.at[t, j], y_r.at[t, j], dev(z, xh, None, c * 2 + xl))
                for j, c in enumerate(columns)
            ]
            got_y[b, y] = proj[b, y]

    def add_y(*turns):
        for t in turns:
            b = order[t]
            for copy in to_y[t]:
                copy.wait_recv()
            sums[b] = jnp.sum(f32(got_y[b]), axis=0)
            half_sum[b] = sums[b, 1 - xl].astype(BF16)
            to_x[t] = send(
                half_sum.at[b], got_x.at[b], x_s.at[t], x_r.at[t], dev(z, xh, None, y * 2 + 1 - xl)
            )

    def add_x(*turns):
        for t in turns:
            b = order[t]
            to_x[t].wait_recv()
            total = (sums[b, xl] + f32(got_x[b])).astype(BF16)
            if t == 0:
                blocks[z] = total
            else:
                summed[b] = total
                to_block[t] = send(
                    summed.at[b], blocks.at[z], b_s.at[t - 1], b_r.at[t - 1], dev(b, xh)
                )

    project(0)
    project(1, 2)
    add_y(0)
    for i in range(2):
        moves[i][2].wait_recv()
        moves[i][3].wait_recv()
    project(3)
    add_x(0)
    add_y(1, 2)
    add_x(1, 2)
    add_y(3)
    add_x(3)
    for copy in to_block[1:]:
        copy.wait_recv()
    square = jnp.zeros((16, 1), F32)
    for b in range(4):
        cols = slice(b * 1536, (b + 1) * 1536)
        attended = (f32(stream_ref[:, cols]) + f32(blocks[b])).astype(BF16)
        att_ref[:, cols] = attended
        square += jnp.sum(f32(attended) * f32(attended), axis=-1, keepdims=True)
    normed = f32(att_ref[...]) * lax.rsqrt(square / (2 * half) + 1e-05) * gain_ref[...]
    nrm[0] = normed[:, :half].astype(BF16)
    nrm[1] = normed[:, half:].astype(BF16)
    send_nrm = send(nrm.at[1 - core], nsib, pre_s.at[3], pre_r.at[3], sib)
    send_nrm.wait_recv()

    dispatches = [None] * NC
    shares = [[] for _ in range(NC)]

    def dispatch(c):
        cols = pl.ds(STARTS[c], WIDTHS[c])
        picked = dot(match_own, nrm[core, :, cols]) + dot(match_sib, nsib[:, cols])
        disp[c][...] = picked.astype(BF16).reshape(8, 16, WIDTHS[c])
        dispatches[c] = [
            send(disp[c].at[e], rows[c].at[own, exp], disp_s.at[c, j], disp_r.at[c, j], dev(z, xh, None, e))
            for j, e in enumerate(peers)
        ]
        rows[c][own, exp] = disp[c][exp]

    def row_view(c):
        def view(block, piece):
            if piece is None:
                return rows[c].at[block]
            return rows[c].at[block, pl.ds(piece * 4, 4)]

        return view

    gather = [spread(row_view(c), ga_s.at[c], ga_r.at[c]) for c in range(NC)]

    def share(c, a):
        j = len(shares[c])
        pair = pl.ds(a * 2, 2)
        shares[c].append(send(rows[c].at[pair], rows_sib[c].at[pair], sib_s.at[c, j], sib_r.at[c, j], sib))

    def gather_a(c):
        for copy in dispatches[c]:
            copy.wait_recv()
        gather[c][0]()

    def gather_b(c):
        gather[c][1]()
        share(c, z)

    def gather_c(c):
        gather[c][2]()

    def gather_d(c):
        gather[c][3]()
        share(c, down_z)
        share(c, up_z)
        share(c, far_z)

    def term(source, c, base, i):
        lhs = source[c][pl.ds(i * 2, 2)].reshape(256, WIDTHS[c])
        return dot(lhs, wgu[pl.ds(pl.multiple_of(base + STARTS[c], 128), WIDTHS[c]), :])

    def multiply_own(c):
        if c == 0:
            loads[1].wait()
            loads[2].wait()

        def body(i, carry):
            value = term(rows, c, core * half, i)
            acc[i] = value if c == 0 else acc[i] + value
            return carry

        lax.fori_loop(0, 4, body, 0)

    sent_hidden = []

    def multiply_sib(c):
        for copy in shares[c]:
            copy.wait_recv()

        def body(i, carry):
            acc[i] += term(rows_sib, c, (1 - core) * half, i)
            return carry

        if c < NC - 1:
            lax.fori_loop(0, 4, body, 0)
            return
        for i in range(4):
            value = acc[i] + term(rows_sib, c, (1 - core) * half, i)
            gate_part, up_part = value[:, :384], value[:, 384:]
            hid[i, :, core_cols] = (gate_part / (1.0 + jnp.exp(-gate_part)) * up_part).astype(BF16)
            view = hid.at[i, :, core_cols]
            sent_hidden.append(send(view, view, hid_s.at[i], hid_r.at[i], sib))

    dispatch(0)
    dispatch(1)
    staged(
        NC,
        (0, gather_a),
        (-2, dispatch),
        (1, gather_b),
        (2, gather_c),
        (3, gather_d),
        (3, multiply_own),
        (4, multiply_sib),
    )
    loads[3].wait()
    send_down.wait_recv()

    reduce = [[None] * 8 for _ in range(NC)]
    returns = [None] * NC

    def send_sum(c, k, src, dst, device):
        reduce[c][k] = send(src, dst, rs_s.at[c, k], rs_r.at[c, k], device)

    def reduce_a(c):
        def body(i, carry):
            out = dot(hid[i], wd[:, STARTS[c] : STARTS[c] + WIDTHS[c]])
            part[c][pl.ds(i * 2, 2)] = out.astype(BF16).reshape(2, 8, 16, WIDTHS[c])
            return carry

        if c == 0:
            for i in range(4):
                sent_hidden[i].wait_recv()
                body(i, 0)
        else:
            lax.fori_loop(0, 4, body, 0)
        send_sum(c, 0, part[c].at[blk(up_z, 1 - xh)], got1[c].at[0], zp)
        send_sum(c, 1, part[c].at[blk(down_z, 1 - xh)], got1[c].at[1], zm)
        send_sum(c, 2, part[c].at[blk(far_z, 1 - xh)], got2[c], xp)

    def reduce_b(c):
        reduce[c][2].wait_recv()
        block = blk(far_z, xh)
        part[c][block] = (f32(part[c][block]) + f32(got2[c][...])).astype(BF16)
        send_sum(c, 3, part[c].at[block, pl.ds(0, 4)], got4[c].at[0], zm)
        send_sum(c, 4, part[c].at[block, pl.ds(4, 4)], got4[c].at[1], zp)
        reduce[c][0].wait_recv()
        reduce[c][1].wait_recv()
        block = blk(z, 1 - xh)
        part[c][block] = (f32(part[c][block]) + f32(got1[c][0]) + f32(got1[c][1])).astype(BF16)
        send_sum(c, 5, part[c].at[block], got3[c], xp)

    def reduce_c(c):
        reduce[c][3].wait_recv()
        block = blk(down_z, xh)
        part[c][block, 0:4] = (f32(part[c][block, 0:4]) + f32(got4[c][0])).astype(BF16)
        send_sum(c, 6, part[c].at[block], got5[c].at[0], zm)
        reduce[c][4].wait_recv()
        block = blk(up_z, xh)
        part[c][block, 4:8] = (f32(part[c][block, 4:8]) + f32(got4[c][1])).astype(BF16)
        send_sum(c, 7, part[c].at[block], got5[c].at[1], zp)

    def reduce_d(c):
        for k in (5, 6, 7):
            reduce[c][k].wait_recv()
        final[c][...] = (f32(part[c][own]) + f32(got3[c][...]) + (f32(got5[c][0]) + f32(got5[c][1]))).astype(BF16)
        returns[c] = [
            send(final[c].at[e], back[c].at[exp], back_s.at[c, j], back_r.at[c, j], dev(z, xh, None, e))
            for j, e in enumerate(peers)
        ]
        back[c][exp] = final[c][exp]

    def weigh(weight, values):
        return jnp.dot(weight, values, precision=lax.Precision.HIGHEST, preferred_element_type=F32)

    def combine(c):
        for copy in returns[c]:
            copy.wait_recv()
        values = f32(back[c][...].reshape(128, WIDTHS[c]))
        contrib_sib[:, STARTS[c] : STARTS[c] + WIDTHS[c]] = weigh(weight_sib, values)
        cols = pl.ds(pl.multiple_of(core * half + STARTS[c], 128), WIDTHS[c])
        out_ref[:, cols] = (f32(att_ref[:, cols]) + weigh(weight_own, values)).astype(BF16)

    staged(NC, (0, reduce_a), (1, reduce_b), (2, reduce_c), (3, reduce_d), (4, combine))

    last = send(contrib_sib, contrib, pre_s.at[4], pre_r.at[4], sib)
    last.wait_recv()
    out_ref[:, sib_half] = (f32(att_ref[:, sib_half]) + contrib[...]).astype(BF16)
    for copy in started:
        copy.wait_send()


def on_device(
    stream,
    queries,
    key_head_rows,
    value_head_rows,
    block_order,
    out_weight,
    norm_gain,
    gate_weight,
    up_weight,
    down_weight,
    expert_ids,
    expert_weights,
):
    d = stream.shape[1]
    half = d // 2
    vmem = pl.BlockSpec(memory_space=pltpu.VMEM)
    smem = pl.BlockSpec(memory_space=pltpu.SMEM)
    anyspace = pl.BlockSpec(memory_space=pl.ANY)

    def per_chunk(*shape):
        return [pltpu.VMEM(shape + (width,), BF16) for width in WIDTHS]

    def sems(*shapes):
        return [pltpu.SemaphoreType.DMA(shape) for shape in shapes for _ in range(2)]

    return pl.pallas_call(
        layer_kernel,
        out_shape=(jax.ShapeDtypeStruct(stream.shape, BF16),) * 2,
        in_specs=[vmem, vmem, vmem, smem, anyspace, vmem, vmem, vmem, vmem, anyspace, anyspace, anyspace],
        out_specs=(vmem, vmem),
        scratch_shapes=[
            pltpu.VMEM((2, 2, 4, 2, 128, 128), BF16),
            pltpu.VMEM((1, 2048), jnp.int32),
            pltpu.VMEM((128, 2048), F32),
            pltpu.VMEM((1024, 1536), BF16),
            pltpu.VMEM((2, 4, 128, 512), BF16),
            pltpu.VMEM((4, 4, 2, 16, 1536), BF16),
            pltpu.VMEM((4, 4, 2, 16, 1536), BF16),
            pltpu.VMEM((4, 2, 16, 1536), F32),
            pltpu.VMEM((4, 16, 1536), BF16),
            pltpu.VMEM((4, 16, 1536), BF16),
            pltpu.VMEM((4, 16, 1536), BF16),
            pltpu.VMEM((4, 16, 1536), BF16),
            pltpu.VMEM((d, 768), BF16),
            pltpu.VMEM((768, half), BF16),
            pltpu.VMEM((8, 128), F32),
            pltpu.VMEM((8, 128), F32),
            pltpu.VMEM((2, 16, half), BF16),
            pltpu.VMEM((16, half), BF16),
            per_chunk(8, 16),
            per_chunk(8, 8, 16),
            per_chunk(8, 8, 16),
            pltpu.VMEM((4, 256, 768), F32),
            pltpu.VMEM((4, 256, 768), BF16),
            per_chunk(8, 8, 16),
            per_chunk(2, 8, 16),
            per_chunk(8, 16),
            per_chunk(8, 16),
            per_chunk(2, 4, 16),
            per_chunk(2, 8, 16),
            per_chunk(8, 16),
            per_chunk(8, 16),
            pltpu.VMEM((16, half), F32),
            pltpu.VMEM((16, half), F32),
            pltpu.SemaphoreType.DMA((4,)),
        ]
        + sems(
            (5,), (9,), (8,), (2, 4), (4, 3), (4,), (3,),
            (NC, 7), (NC, 8), (NC, 4), (4,), (NC, 8), (NC, 7),
        ),
        compiler_params=pltpu.CompilerParams(
            collective_id=0, has_side_effects=True, vmem_limit_bytes=VMEM_LIMIT
        ),
        cost_estimate=pl.CostEstimate(
            flops=2 * 3 * 1024 * d * 384 + 4 * 1024 * 128 * 2048 + 2 * 1024 * 1024 * 768,
            bytes_accessed=3 * d * 384 * 2,
            transcendentals=1024 * 2048 + 1024 * 384,
        ),
        name="layer",
    )(
        queries, key_head_rows, value_head_rows, block_order, out_weight, stream, norm_gain.reshape(1, d),
        expert_ids.T, expert_weights.T, gate_weight, up_weight, down_weight,
    )


def solution(mesh):
    in_specs = (
        P(("ctx", "exp"), None),
        P("ctx", "exp"),
        P("ctx", "exp"),
        P("ctx", "exp"),
        P(),
        P("exp", "ctx"),
        P(),
        P("exp", None, "ctx"),
        P("exp", None, "ctx"),
        P("exp", "ctx", None),
        P(("ctx", "exp"), None),
        P(("ctx", "exp"), None),
    )
    out_specs = (P(("ctx", "exp"), None), P(("ctx", "exp"), None))
    return jax.shard_map(
        on_device, mesh=mesh, in_specs=in_specs, out_specs=out_specs, check_vma=False
    )
```

```python
import jax
import jax.numpy as jnp
from jax import lax
from jax.experimental import pallas as pl
from jax.experimental.pallas import tpu as pltpu
from jax.sharding import PartitionSpec as P

HEAD = 128
MESH = pl.DeviceIdType.MESH
VMEM_LIMIT = 62 * 2**20
SPLITS = ((1024, 1024, 1024), (1024, 1024, 1024))
UNITS = tuple(
    (part, sum(split[:c]), width) for part, split in enumerate(SPLITS) for c, width in enumerate(split)
)
FIRST = len(SPLITS[0])
NC = len(UNITS)
BF16, F32 = jnp.bfloat16, jnp.float32


def f32(value):
    return value.astype(F32)


def dot(a, b):
    return jnp.dot(a, b, preferred_element_type=F32)


def remote(src, dst, send, recv, device):
    return pltpu.make_async_remote_copy(
        src_ref=src, dst_ref=dst, send_sem=send, recv_sem=recv, device_id=device, device_id_type=MESH
    )


def greet(devices):
    barrier = pltpu.get_barrier_semaphore()
    for device in devices:
        pl.semaphore_signal(barrier, inc=1, device_id=device, device_id_type=MESH)
    pl.semaphore_wait(barrier, len(devices))


def slot_match(meta, core, exp):
    row = lax.broadcasted_iota(jnp.int32, (128, 128), 0)
    lane = lax.broadcasted_iota(jnp.int32, (128, 128), 1)
    expert = f32(lax.rem(exp + row // 16, 8))
    first = (meta[0:1, :] == expert) & (lane < 16)
    second = (meta[1:2, :] == expert) & (lane < 16)
    named = jnp.where(first | second, 1.0, 0.0)
    earlier = jnp.where(row < lane, 1.0, 0.0)
    rank = dot(named.astype(BF16), earlier.astype(BF16))
    slot = f32(lax.rem(row, 8))
    mine = lax.rem(row // 8, 2) == core
    match = jnp.where((rank == slot) & mine, named, 0.0)
    weight = match * jnp.where(first, meta[2:3, :], meta[3:4, :])
    return match[:, :16].astype(BF16), weight.T[:16, :]


def staged(count, *stages):
    for step in range(count + max(late for late, _ in stages)):
        for late, stage in stages:
            if 0 <= step - late < count:
                stage(step - late)


def layer_kernel(
    q_ref, k_ref, v_ref, order_ref, proj_ref, stream_ref, gain_ref, ids_ref, mix_ref,
    gate_ref, up_ref, down_ref, att_ref, out_ref,
    kv, kpos, bias, wcat, heads, proj, got_y, sums, half_sum, got_x, got_pair, pair_sum, summed, blocks,
    wgu, wd, meta, meta_sib, nrm, nsib, disp, rows, rows_sib, acc, hid, part,
    got1, got2, got3, got4, got5, final, back, contrib, contrib_sib, contrib_own,
    load_sem, pre_s, pre_r, kv_s, kv_r, w_s, w_r, h_s, h_r, y_s, y_r, x_s, x_r, b_s, b_r,
    disp_s, disp_r, ga_s, ga_r, sib_s, sib_r, hid_s, hid_r, rs_s, rs_r, back_s, back_r,
):
    ctx = lax.axis_index("ctx")
    exp = lax.axis_index("exp")
    z, xh, core = ctx // 4, lax.rem(ctx // 2, 2), lax.rem(ctx, 2)
    y, xl = exp // 2, lax.rem(exp, 2)
    up_z, down_z, far_z = lax.rem(z + 1, 4), lax.rem(z + 3, 4), lax.rem(z + 2, 4)
    half = sum(SPLITS[0])

    def dev(a, b, c=None, e=None):
        return (a * 4 + b * 2 + (core if c is None else c), exp if e is None else e)

    def blk(a, b):
        return a * 2 + b

    zp, zm, xp, sib = dev(up_z, xh), dev(down_z, xh), dev(z, 1 - xh), dev(z, xh, 1 - core)
    peers = [lax.rem(exp + j, 8) for j in range(1, 8)]
    columns = [lax.rem(y + j, 4) for j in range(1, 4)]
    own = blk(z, xh)
    far = dev(far_z, xh)
    started = []

    def send(src, dst, s, r, device):
        copy = remote(src, dst, s, r, device)
        copy.start()
        started.append(copy)
        return copy

    def spread(view, s, r):
        copies = [None] * 8

        def forward(k, block, device, piece=None):
            ref = view(block, piece)
            copies[k] = send(ref, ref, s.at[k], r.at[k], device)

        def first():
            forward(0, own, zp)
            forward(1, own, zm)
            forward(2, own, xp)

        def second():
            copies[0].wait_recv()
            forward(3, blk(down_z, xh), zp, 0)
            copies[1].wait_recv()
            forward(4, blk(up_z, xh), zm, 1)
            copies[2].wait_recv()
            forward(5, blk(z, 1 - xh), zp)
            forward(6, blk(z, 1 - xh), zm)

        def third():
            copies[3].wait_recv()
            copies[4].wait_recv()
            forward(7, blk(far_z, xh), xp)

        def fourth():
            copies[5].wait_recv()
            copies[6].wait_recv()
            copies[7].wait_recv()

        return first, second, third, fourth

    def proj_cols(a, b):
        return pl.ds(pl.multiple_of((a * 2 + b) * 384, 128), 384)

    own_cols = proj_cols(xh, core)
    core_cols = pl.ds(pl.multiple_of(core * 384, 128), 384)
    core_half = pl.ds(pl.multiple_of(core * half, 128), half)
    sib_half = pl.ds(pl.multiple_of((1 - core) * half, 128), half)
    loads = [
        pltpu.make_async_copy(proj_ref, wcat.at[:, own_cols], load_sem.at[0]),
        pltpu.make_async_copy(gate_ref.at[0], wgu.at[:, pl.ds(0, 384)], load_sem.at[1]),
        pltpu.make_async_copy(up_ref.at[0], wgu.at[:, pl.ds(384, 384)], load_sem.at[2]),
        pltpu.make_async_copy(down_ref.at[0, :, core_half], wd.at[core_cols], load_sem.at[3]),
    ]
    loads[0].start()
    kv[core, xh, z, 0] = k_ref[...]
    kv[core, xh, z, 1] = v_ref[...]
    meta[...] = jnp.zeros_like(meta)
    meta[0:2, 0:16] = f32(ids_ref[...])
    meta[2:4, 0:16] = mix_ref[...]
    greet([zp, zm, far, xp, sib] + [dev(z, xh, None, e) for e in peers])

    def send_kv(k, a, b, device):
        return send(kv.at[core, a, b], kv.at[core, a, b], kv_s.at[k], kv_r.at[k], device)

    from_x = send_kv(0, xh, z, xp)
    column = [send_kv(1 + j, xh, z, device) for j, device in enumerate((zp, zm, far))]
    piece = 256
    send_w = [
        send(
            proj_ref.at[pl.ds(i * piece, piece)], wcat.at[pl.ds(i * piece, piece), own_cols],
            w_s.at[i], w_r.at[i], xp,
        )
        for i in range(4)
    ]
    send_w_sib = send(proj_ref, wcat.at[:, own_cols], pre_s.at[0], pre_r.at[0], sib)
    send_meta = send(meta, meta_sib, pre_s.at[1], pre_r.at[1], sib)
    from_x.wait_recv()
    column += [send_kv(4 + j, 1 - xh, z, device) for j, device in enumerate((zp, zm, far))]
    lane = lax.broadcasted_iota(jnp.int32, (1, 128), 1)
    for slot in range(16):
        place = slot % 4 * 4 + slot // 4 % 2 * 2 + slot // 8
        first = jnp.where(lane < 64, order_ref[2 * place], order_ref[2 * place + 1])
        kpos[:, slot * 128 : (slot + 1) * 128] = first * 64 + lax.rem(lane, 64)
    row = lax.broadcasted_iota(jnp.int32, (128, 1), 0)
    qpos = jnp.where(row < 64, order_ref[2 * ctx], order_ref[2 * ctx + 1]) * 64 + lax.rem(row, 64)
    bias[...] = jnp.where(kpos[...] <= qpos, 0.0, -1e30)
    match_own, weight_own = slot_match(meta[...], core, exp)
    for copy in column[:3]:
        copy.wait_recv()
    share_kv = [send(kv.at[core, xh], kv.at[core, xh], kv_s.at[7], kv_r.at[7], sib)]
    send_meta.wait_recv()
    match_sib, weight_sib = slot_match(meta_sib[...], 1 - core, exp)
    for copy in column[3:]:
        copy.wait_recv()
    share_kv.append(send(kv.at[core, 1 - xh], kv.at[core, 1 - xh], kv_s.at[8], kv_r.at[8], sib))
    for copy in share_kv:
        copy.wait_recv()

    scale = HEAD ** (-0.5) * 1.4426950408889634

    def attend(part_of):
        def body(i, carry):
            pair = q_ref[:, pl.ds(pl.multiple_of(part_of * 512 + i * 256, 128), 256)]
            q = jnp.concatenate([pair[:, :128], pair[:, 128:]], axis=0)
            keys = kv[:, :, :, 0].reshape(2048, HEAD)
            values = kv[:, :, :, 1].reshape(2048, HEAD)
            logits = lax.dot_general(q, keys, (((1,), (1,)), ((), ())), preferred_element_type=F32)
            logits = logits.reshape(2, 128, 2048) * scale + bias[...][None]
            expd = jnp.exp2(logits - jnp.max(logits, axis=-1, keepdims=True))
            total = jnp.sum(expd, axis=-1, keepdims=True)
            weighted = dot(expd.astype(BF16).reshape(256, 2048), values)
            result = (weighted.reshape(2, 128, HEAD) / total).astype(BF16)
            heads[part_of, z, :, pl.ds(pl.multiple_of(i * 256, 128), 256)] = jnp.concatenate(
                [result[0], result[1]], axis=1
            )
            return carry

        lax.fori_loop(0, 2, body, 0)

    def send_heads(i, k, a, rows_of, device):
        view = heads.at[i, a, rows_of]
        return send(view, view, h_s.at[i, k], h_r.at[i, k], device)

    moves = []
    for i in range(2):
        attend(i)
        moves.append([send_heads(i, k, z, pl.ds(0, 128), device) for k, device in enumerate((zp, zm))])
    for load in loads[1:]:
        load.start()
    send_down = send(down_ref.at[0, :, sib_half], wd.at[core_cols], pre_s.at[2], pre_r.at[2], sib)
    far_w = []
    for i in range(4):
        send_w[i].wait_recv()
        view = wcat.at[pl.ds(i * piece, piece), proj_cols(1 - xh, core)]
        far_w.append(send(view, view, w_s.at[4 + i], w_r.at[4 + i], sib))
    for i in range(2):
        moves[i][0].wait_recv()
        moves[i].append(send_heads(i, 2, down_z, pl.ds(0, 64), zp))
        moves[i][1].wait_recv()
        moves[i].append(send_heads(i, 3, up_z, pl.ds(64, 64), zm))
    loads[0].wait()
    send_w_sib.wait_recv()
    for copy in far_w:
        copy.wait_recv()

    order = [z, down_z, up_z, far_z]
    to_y = [None] * 4
    to_x = [None] * 4
    to_block = [None] * 4
    x_first = (1, 3)

    def project(*turns):
        places = [order[t] for t in turns]
        product = 0.0
        for i in range(2):
            lhs = jnp.concatenate([heads[i, b] for b in places], axis=0)
            product += dot(lhs, wcat[i * 512 : (i + 1) * 512, :])
        for n, (t, b) in enumerate(zip(turns, places)):
            proj[b] = product[n * 128 : (n + 1) * 128].astype(BF16).reshape(4, 2, 16, 1536)
            if t in x_first:
                to_x[t] = send(
                    proj.at[b, :, 1 - xl], got_pair.at[b], x_s.at[t], x_r.at[t],
                    dev(z, xh, None, y * 2 + 1 - xl),
                )
                continue
            to_y[t] = [
                send(proj.at[b, c], got_y.at[b, y], y_s.at[t, j], y_r.at[t, j], dev(z, xh, None, c * 2 + xl))
                for j, c in enumerate(columns)
            ]
            got_y[b, y] = proj[b, y]

    def add_first(*turns):
        for t in turns:
            b = order[t]
            if t in x_first:
                to_x[t].wait_recv()
                pair_sum[b] = (f32(proj[b, :, xl]) + f32(got_pair[b])).astype(BF16)
                to_y[t] = [
                    send(
                        pair_sum.at[b, c], got_y.at[b, y, 0], y_s.at[t, j], y_r.at[t, j],
                        dev(z, xh, None, c * 2 + xl),
                    )
                    for j, c in enumerate(columns)
                ]
                got_y[b, y, 0] = pair_sum[b, y]
                continue
            for copy in to_y[t]:
                copy.wait_recv()
            sums[b] = jnp.sum(f32(got_y[b]), axis=0)
            half_sum[b] = sums[b, 1 - xl].astype(BF16)
            to_x[t] = send(
                half_sum.at[b], got_x.at[b], x_s.at[t], x_r.at[t], dev(z, xh, None, y * 2 + 1 - xl)
            )

    def add_second(*turns):
        for t in turns:
            b = order[t]
            if t in x_first:
                for copy in to_y[t]:
                    copy.wait_recv()
                total = jnp.sum(f32(got_y[b, :, 0]), axis=0).astype(BF16)
            else:
                to_x[t].wait_recv()
                total = (sums[b, xl] + f32(got_x[b])).astype(BF16)
            if t == 0:
                blocks[z] = total
            else:
                summed[b] = total
                to_block[t] = send(
                    summed.at[b], blocks.at[z], b_s.at[t - 1], b_r.at[t - 1], dev(b, xh)
                )

    project(0)
    project(1, 2)
    add_first(0)
    for i in range(2):
        moves[i][2].wait_recv()
        moves[i][3].wait_recv()
    project(3)
    add_second(0)
    add_first(1, 2)
    add_second(1, 2)
    add_first(3)
    add_second(3)
    for copy in to_block[1:]:
        copy.wait_recv()
    square = jnp.zeros((16, 1), F32)
    for b in range(4):
        cols = slice(b * 1536, (b + 1) * 1536)
        attended = (f32(stream_ref[:, cols]) + f32(blocks[b])).astype(BF16)
        att_ref[:, cols] = attended
        square += jnp.sum(f32(attended) * f32(attended), axis=-1, keepdims=True)
    normed = f32(att_ref[...]) * lax.rsqrt(square / (2 * half) + 1e-05) * gain_ref[...]
    nrm[0] = normed[:, :half].astype(BF16)
    nrm[1] = normed[:, half:].astype(BF16)
    send_nrm = send(nrm.at[1 - core], nsib, pre_s.at[3], pre_r.at[3], sib)
    send_nrm.wait_recv()

    dispatches = [None] * NC
    shares = [[] for _ in range(NC)]

    def dispatch(c):
        half_of, start, width = UNITS[c]
        cols = pl.ds(start, width)
        slots = slice(half_of * 64, half_of * 64 + 64)
        picked = dot(match_own[slots], nrm[core, :, cols]) + dot(match_sib[slots], nsib[:, cols])
        disp[c][...] = picked.astype(BF16).reshape(4, 16, width)
        dispatches[c] = [
            send(
                disp[c].at[j], rows[c].at[own, j], disp_s.at[c, j], disp_r.at[c, j],
                dev(z, xh, None, lax.rem(exp + half_of * 4 + j, 8)),
            )
            for j in range(4)
            if half_of * 4 + j > 0
        ]
        if half_of == 0:
            rows[c][own, 0] = disp[c][0]

    def row_view(c):
        def view(block, piece):
            if piece is None:
                return rows[c].at[block]
            return rows[c].at[block, pl.ds(piece * 2, 2)]

        return view

    gather = [spread(row_view(c), ga_s.at[c], ga_r.at[c]) for c in range(NC)]

    def share(c, a):
        j = len(shares[c])
        pair = pl.ds(a * 2, 2)
        shares[c].append(send(rows[c].at[pair], rows_sib[c].at[pair], sib_s.at[c, j], sib_r.at[c, j], sib))

    def gather_a(c):
        for copy in dispatches[c]:
            copy.wait_recv()
        gather[c][0]()

    def gather_b(c):
        gather[c][1]()
        share(c, z)

    def gather_c(c):
        gather[c][2]()

    def gather_d(c):
        gather[c][3]()
        share(c, down_z)
        share(c, up_z)
        share(c, far_z)

    def term(source, c, base, i):
        _, start, width = UNITS[c]
        lhs = source[c][pl.ds(i * 4, 4)].reshape(256, width)
        return dot(lhs, wgu[pl.ds(pl.multiple_of(base + start, 128), width), :])

    def multiply_own(c):
        if c == 0:
            loads[1].wait()
            loads[2].wait()
        half_of, start, _ = UNITS[c]

        def body(i, carry):
            value = term(rows, c, core * half, i)
            acc[half_of, i] = value if start == 0 else acc[half_of, i] + value
            return carry

        lax.fori_loop(0, 2, body, 0)

    sent_hidden = [[], []]

    def multiply_sib(c):
        for copy in shares[c]:
            copy.wait_recv()
        half_of, start, width = UNITS[c]

        def body(i, carry):
            acc[half_of, i] += term(rows_sib, c, (1 - core) * half, i)
            return carry

        if start + width < half:
            lax.fori_loop(0, 2, body, 0)
            return
        for i in range(2):
            value = acc[half_of, i] + term(rows_sib, c, (1 - core) * half, i)
            gate_part, up_part = value[:, :384], value[:, 384:]
            hid[half_of, i, :, core_cols] = (gate_part / (1.0 + jnp.exp(-gate_part)) * up_part).astype(BF16)
            view = hid.at[half_of, i, :, core_cols]
            sent_hidden[half_of].append(
                send(view, view, hid_s.at[half_of, i], hid_r.at[half_of, i], sib)
            )

    reduce = [[None] * 8 for _ in range(NC)]
    returns = [None] * NC

    def send_sum(c, k, src, dst, device):
        reduce[c][k] = send(src, dst, rs_s.at[c, k], rs_r.at[c, k], device)

    def reduce_a(c):
        half_of, start, width = UNITS[c]

        def body(i, carry):
            out = dot(hid[half_of, i], wd[:, start : start + width])
            part[c][pl.ds(i * 4, 4)] = out.astype(BF16).reshape(4, 4, 16, width)
            return carry

        if c == 0:
            loads[3].wait()
            send_down.wait_recv()
        if start == 0:
            for i in range(2):
                sent_hidden[half_of][i].wait_recv()
                body(i, 0)
        else:
            lax.fori_loop(0, 2, body, 0)
        send_sum(c, 0, part[c].at[blk(up_z, 1 - xh)], got1[c].at[0], zp)
        send_sum(c, 1, part[c].at[blk(down_z, 1 - xh)], got1[c].at[1], zm)
        send_sum(c, 2, part[c].at[blk(far_z, 1 - xh)], got2[c], xp)

    def reduce_b(c):
        reduce[c][2].wait_recv()
        block = blk(far_z, xh)
        part[c][block] = (f32(part[c][block]) + f32(got2[c][...])).astype(BF16)
        send_sum(c, 3, part[c].at[block, pl.ds(0, 2)], got4[c].at[0], zm)
        send_sum(c, 4, part[c].at[block, pl.ds(2, 2)], got4[c].at[1], zp)
        reduce[c][0].wait_recv()
        reduce[c][1].wait_recv()
        block = blk(z, 1 - xh)
        part[c][block] = (f32(part[c][block]) + f32(got1[c][0]) + f32(got1[c][1])).astype(BF16)
        send_sum(c, 5, part[c].at[block], got3[c], xp)

    def reduce_c(c):
        reduce[c][3].wait_recv()
        block = blk(down_z, xh)
        part[c][block, 0:2] = (f32(part[c][block, 0:2]) + f32(got4[c][0])).astype(BF16)
        send_sum(c, 6, part[c].at[block], got5[c].at[0], zm)
        reduce[c][4].wait_recv()
        block = blk(up_z, xh)
        part[c][block, 2:4] = (f32(part[c][block, 2:4]) + f32(got4[c][1])).astype(BF16)
        send_sum(c, 7, part[c].at[block], got5[c].at[1], zp)

    def reduce_d(c):
        for k in (5, 6, 7):
            reduce[c][k].wait_recv()
        final[c][...] = (f32(part[c][own]) + f32(got3[c][...]) + (f32(got5[c][0]) + f32(got5[c][1]))).astype(BF16)
        half_of = UNITS[c][0]
        returns[c] = [
            send(
                final[c].at[j], back[c].at[j], back_s.at[c, j], back_r.at[c, j],
                dev(z, xh, None, lax.rem(exp + 8 - half_of * 4 - j, 8)),
            )
            for j in range(4)
            if half_of * 4 + j > 0
        ]
        if half_of == 0:
            back[c][0] = final[c][0]

    def weigh(weight, values):
        return jnp.dot(weight, values, precision=lax.Precision.HIGHEST, preferred_element_type=F32)

    def combine(c):
        for copy in returns[c]:
            copy.wait_recv()
        half_of, start, width = UNITS[c]
        values = f32(back[c][...].reshape(64, width))
        slots = slice(half_of * 64, half_of * 64 + 64)
        for_sib, for_own = weigh(weight_sib[:, slots], values), weigh(weight_own[:, slots], values)
        cols = slice(start, start + width)
        if half_of == 0:
            contrib_sib[:, cols] = for_sib
            contrib_own[:, cols] = for_own
            return
        contrib_sib[:, cols] += for_sib
        place = pl.ds(pl.multiple_of(core * half + start, 128), width)
        out_ref[:, place] = (f32(att_ref[:, place]) + (contrib_own[:, cols] + for_own)).astype(BF16)

    dispatch(0)
    dispatch(1)
    staged(
        NC,
        (0, gather_a),
        (-2, dispatch),
        (1, gather_b),
        (2, gather_c),
        (3, gather_d),
        (3, multiply_own),
        (4, multiply_sib),
        (FIRST + 3, reduce_a),
        (FIRST + 4, reduce_b),
        (FIRST + 5, reduce_c),
        (FIRST + 6, reduce_d),
        (FIRST + 7, combine),
    )

    last = send(contrib_sib, contrib, pre_s.at[4], pre_r.at[4], sib)
    last.wait_recv()
    out_ref[:, sib_half] = (f32(att_ref[:, sib_half]) + contrib[...]).astype(BF16)
    for copy in started:
        copy.wait_send()


def on_device(
    stream,
    queries,
    key_head_rows,
    value_head_rows,
    block_order,
    out_weight,
    norm_gain,
    gate_weight,
    up_weight,
    down_weight,
    expert_ids,
    expert_weights,
):
    d = stream.shape[1]
    half = d // 2
    vmem = pl.BlockSpec(memory_space=pltpu.VMEM)
    smem = pl.BlockSpec(memory_space=pltpu.SMEM)
    anyspace = pl.BlockSpec(memory_space=pl.ANY)

    def per_chunk(*shape):
        return [pltpu.VMEM(shape + (width,), BF16) for _, _, width in UNITS]

    def sems(*shapes):
        return [pltpu.SemaphoreType.DMA(shape) for shape in shapes for _ in range(2)]

    return pl.pallas_call(
        layer_kernel,
        out_shape=(jax.ShapeDtypeStruct(stream.shape, BF16),) * 2,
        in_specs=[vmem, vmem, vmem, smem, anyspace, vmem, vmem, vmem, vmem, anyspace, anyspace, anyspace],
        out_specs=(vmem, vmem),
        scratch_shapes=[
            pltpu.VMEM((2, 2, 4, 2, 128, 128), BF16),
            pltpu.VMEM((1, 2048), jnp.int32),
            pltpu.VMEM((128, 2048), F32),
            pltpu.VMEM((1024, 1536), BF16),
            pltpu.VMEM((2, 4, 128, 512), BF16),
            pltpu.VMEM((4, 4, 2, 16, 1536), BF16),
            pltpu.VMEM((4, 4, 2, 16, 1536), BF16),
            pltpu.VMEM((4, 2, 16, 1536), F32),
            pltpu.VMEM((4, 16, 1536), BF16),
            pltpu.VMEM((4, 16, 1536), BF16),
            pltpu.VMEM((4, 4, 16, 1536), BF16),
            pltpu.VMEM((4, 4, 16, 1536), BF16),
            pltpu.VMEM((4, 16, 1536), BF16),
            pltpu.VMEM((4, 16, 1536), BF16),
            pltpu.VMEM((d, 768), BF16),
            pltpu.VMEM((768, half), BF16),
            pltpu.VMEM((8, 128), F32),
            pltpu.VMEM((8, 128), F32),
            pltpu.VMEM((2, 16, half), BF16),
            pltpu.VMEM((16, half), BF16),
            per_chunk(4, 16),
            per_chunk(8, 4, 16),
            per_chunk(8, 4, 16),
            pltpu.VMEM((2, 2, 256, 768), F32),
            pltpu.VMEM((2, 2, 256, 768), BF16),
            per_chunk(8, 4, 16),
            per_chunk(2, 4, 16),
            per_chunk(4, 16),
            per_chunk(4, 16),
            per_chunk(2, 2, 16),
            per_chunk(2, 4, 16),
            per_chunk(4, 16),
            per_chunk(4, 16),
            pltpu.VMEM((16, half), F32),
            pltpu.VMEM((16, half), F32),
            pltpu.VMEM((16, half), F32),
            pltpu.SemaphoreType.DMA((4,)),
        ]
        + sems(
            (5,), (9,), (8,), (2, 4), (4, 3), (4,), (3,),
            (NC, 4), (NC, 8), (NC, 4), (2, 2), (NC, 8), (NC, 4),
        ),
        compiler_params=pltpu.CompilerParams(
            collective_id=0, has_side_effects=True, vmem_limit_bytes=VMEM_LIMIT
        ),
        cost_estimate=pl.CostEstimate(
            flops=2 * 3 * 1024 * d * 384 + 4 * 1024 * 128 * 2048 + 2 * 1024 * 1024 * 768,
            bytes_accessed=3 * d * 384 * 2,
            transcendentals=1024 * 2048 + 1024 * 384,
        ),
        name="layer",
    )(
        queries, key_head_rows, value_head_rows, block_order, out_weight, stream, norm_gain.reshape(1, d),
        expert_ids.T, expert_weights.T, gate_weight, up_weight, down_weight,
    )


def solution(mesh):
    in_specs = (
        P(("ctx", "exp"), None),
        P("ctx", "exp"),
        P("ctx", "exp"),
        P("ctx", "exp"),
        P(),
        P("exp", "ctx"),
        P(),
        P("exp", None, "ctx"),
        P("exp", None, "ctx"),
        P("exp", "ctx", None),
        P(("ctx", "exp"), None),
        P(("ctx", "exp"), None),
    )
    out_specs = (P(("ctx", "exp"), None), P(("ctx", "exp"), None))
    return jax.shard_map(
        on_device, mesh=mesh, in_specs=in_specs, out_specs=out_specs, check_vma=False
    )
```

```python
import jax
import jax.numpy as jnp
from jax import lax
from jax.experimental import pallas as pl
from jax.experimental.pallas import tpu as pltpu
from jax.sharding import PartitionSpec as P

HEAD = 128
MESH = pl.DeviceIdType.MESH
VMEM_LIMIT = 62 * 2**20
SPLITS = ((768, 768, 768, 768), (768, 768, 768, 768))
UNITS = tuple(
    (part, sum(split[:c]), width) for part, split in enumerate(SPLITS) for c, width in enumerate(split)
)
FIRST = len(SPLITS[0])
NC = len(UNITS)
BF16, F32 = jnp.bfloat16, jnp.float32


def f32(value):
    return value.astype(F32)


def dot(a, b):
    return jnp.dot(a, b, preferred_element_type=F32)


def remote(src, dst, send, recv, device):
    return pltpu.make_async_remote_copy(
        src_ref=src, dst_ref=dst, send_sem=send, recv_sem=recv, device_id=device, device_id_type=MESH
    )


def greet(devices):
    barrier = pltpu.get_barrier_semaphore()
    for device in devices:
        pl.semaphore_signal(barrier, inc=1, device_id=device, device_id_type=MESH)
    pl.semaphore_wait(barrier, len(devices))


def slot_match(meta, core, exp):
    row = lax.broadcasted_iota(jnp.int32, (128, 128), 0)
    lane = lax.broadcasted_iota(jnp.int32, (128, 128), 1)
    expert = f32(lax.rem(exp + row // 16, 8))
    first = (meta[0:1, :] == expert) & (lane < 16)
    second = (meta[1:2, :] == expert) & (lane < 16)
    named = jnp.where(first | second, 1.0, 0.0)
    earlier = jnp.where(row < lane, 1.0, 0.0)
    rank = dot(named.astype(BF16), earlier.astype(BF16))
    slot = f32(lax.rem(row, 8))
    mine = lax.rem(row // 8, 2) == core
    match = jnp.where((rank == slot) & mine, named, 0.0)
    weight = match * jnp.where(first, meta[2:3, :], meta[3:4, :])
    return match[:, :16].astype(BF16), weight.T[:16, :]


def staged(count, *stages):
    for step in range(count + max(late for late, _ in stages)):
        for late, stage in stages:
            if 0 <= step - late < count:
                stage(step - late)


def layer_kernel(
    q_ref, k_ref, v_ref, order_ref, proj_ref, stream_ref, gain_ref, ids_ref, mix_ref,
    gate_ref, up_ref, down_ref, att_ref, out_ref,
    kv, kpos, bias, wcat, heads, proj, got_y, sums, half_sum, got_x, got_pair, pair_sum, summed, blocks,
    wgu, wd, meta, meta_sib, nrm, nsib, disp, rows, rows_sib, acc, hid, part,
    got1, got2, got3, got4, got5, final, back, contrib, contrib_sib, contrib_own,
    load_sem, pre_s, pre_r, kv_s, kv_r, w_s, w_r, h_s, h_r, y_s, y_r, x_s, x_r, b_s, b_r,
    disp_s, disp_r, ga_s, ga_r, sib_s, sib_r, hid_s, hid_r, rs_s, rs_r, back_s, back_r,
):
    ctx = lax.axis_index("ctx")
    exp = lax.axis_index("exp")
    z, xh, core = ctx // 4, lax.rem(ctx // 2, 2), lax.rem(ctx, 2)
    y, xl = exp // 2, lax.rem(exp, 2)
    up_z, down_z, far_z = lax.rem(z + 1, 4), lax.rem(z + 3, 4), lax.rem(z + 2, 4)
    half = sum(SPLITS[0])

    def dev(a, b, c=None, e=None):
        return (a * 4 + b * 2 + (core if c is None else c), exp if e is None else e)

    def blk(a, b):
        return a * 2 + b

    zp, zm, xp, sib = dev(up_z, xh), dev(down_z, xh), dev(z, 1 - xh), dev(z, xh, 1 - core)
    peers = [lax.rem(exp + j, 8) for j in range(1, 8)]
    columns = [lax.rem(y + j, 4) for j in range(1, 4)]
    own = blk(z, xh)
    far = dev(far_z, xh)
    started = []

    def send(src, dst, s, r, device):
        copy = remote(src, dst, s, r, device)
        copy.start()
        started.append(copy)
        return copy

    def spread(view, s, r):
        copies = [None] * 8

        def forward(k, block, device, piece=None):
            ref = view(block, piece)
            copies[k] = send(ref, ref, s.at[k], r.at[k], device)

        def first():
            forward(0, own, zp)
            forward(1, own, zm)
            forward(2, own, xp)

        def second():
            copies[0].wait_recv()
            forward(3, blk(down_z, xh), zp, 0)
            copies[1].wait_recv()
            forward(4, blk(up_z, xh), zm, 1)
            copies[2].wait_recv()
            forward(5, blk(z, 1 - xh), zp)
            forward(6, blk(z, 1 - xh), zm)

        def third():
            copies[3].wait_recv()
            copies[4].wait_recv()
            forward(7, blk(far_z, xh), xp)

        def fourth():
            copies[5].wait_recv()
            copies[6].wait_recv()
            copies[7].wait_recv()

        return first, second, third, fourth

    def proj_cols(a, b):
        return pl.ds(pl.multiple_of((a * 2 + b) * 384, 128), 384)

    own_cols = proj_cols(xh, core)
    core_cols = pl.ds(pl.multiple_of(core * 384, 128), 384)
    core_half = pl.ds(pl.multiple_of(core * half, 128), half)
    sib_half = pl.ds(pl.multiple_of((1 - core) * half, 128), half)
    loads = [
        pltpu.make_async_copy(proj_ref, wcat.at[:, own_cols], load_sem.at[0]),
        pltpu.make_async_copy(gate_ref.at[0], wgu.at[:, pl.ds(0, 384)], load_sem.at[1]),
        pltpu.make_async_copy(up_ref.at[0], wgu.at[:, pl.ds(384, 384)], load_sem.at[2]),
        pltpu.make_async_copy(down_ref.at[0, :, core_half], wd.at[core_cols], load_sem.at[3]),
    ]
    loads[0].start()
    kv[core, xh, z, 0] = k_ref[...]
    kv[core, xh, z, 1] = v_ref[...]
    meta[...] = jnp.zeros_like(meta)
    meta[0:2, 0:16] = f32(ids_ref[...])
    meta[2:4, 0:16] = mix_ref[...]
    greet([zp, zm, far, xp, sib] + [dev(z, xh, None, e) for e in peers])

    def send_kv(k, a, b, device):
        return send(kv.at[core, a, b], kv.at[core, a, b], kv_s.at[k], kv_r.at[k], device)

    from_x = send_kv(0, xh, z, xp)
    column = [send_kv(1 + j, xh, z, device) for j, device in enumerate((zp, zm, far))]
    piece = 256
    send_w = [
        send(
            proj_ref.at[pl.ds(i * piece, piece)], wcat.at[pl.ds(i * piece, piece), own_cols],
            w_s.at[i], w_r.at[i], xp,
        )
        for i in range(4)
    ]
    send_w_sib = send(proj_ref, wcat.at[:, own_cols], pre_s.at[0], pre_r.at[0], sib)
    send_meta = send(meta, meta_sib, pre_s.at[1], pre_r.at[1], sib)
    from_x.wait_recv()
    column += [send_kv(4 + j, 1 - xh, z, device) for j, device in enumerate((zp, zm, far))]
    lane = lax.broadcasted_iota(jnp.int32, (1, 128), 1)
    for slot in range(16):
        place = slot % 4 * 4 + slot // 4 % 2 * 2 + slot // 8
        first = jnp.where(lane < 64, order_ref[2 * place], order_ref[2 * place + 1])
        kpos[:, slot * 128 : (slot + 1) * 128] = first * 64 + lax.rem(lane, 64)
    row = lax.broadcasted_iota(jnp.int32, (128, 1), 0)
    qpos = jnp.where(row < 64, order_ref[2 * ctx], order_ref[2 * ctx + 1]) * 64 + lax.rem(row, 64)
    bias[...] = jnp.where(kpos[...] <= qpos, 0.0, -1e30)
    match_own, weight_own = slot_match(meta[...], core, exp)
    for copy in column[:3]:
        copy.wait_recv()
    share_kv = [send(kv.at[core, xh], kv.at[core, xh], kv_s.at[7], kv_r.at[7], sib)]
    send_meta.wait_recv()
    match_sib, weight_sib = slot_match(meta_sib[...], 1 - core, exp)
    for copy in column[3:]:
        copy.wait_recv()
    share_kv.append(send(kv.at[core, 1 - xh], kv.at[core, 1 - xh], kv_s.at[8], kv_r.at[8], sib))
    for copy in share_kv:
        copy.wait_recv()

    scale = HEAD ** (-0.5) * 1.4426950408889634

    def attend(part_of):
        def body(i, carry):
            pair = q_ref[:, pl.ds(pl.multiple_of(part_of * 512 + i * 256, 128), 256)]
            q = jnp.concatenate([pair[:, :128], pair[:, 128:]], axis=0)
            keys = kv[:, :, :, 0].reshape(2048, HEAD)
            values = kv[:, :, :, 1].reshape(2048, HEAD)
            logits = lax.dot_general(q, keys, (((1,), (1,)), ((), ())), preferred_element_type=F32)
            logits = logits.reshape(2, 128, 2048) * scale + bias[...][None]
            expd = jnp.exp2(logits - jnp.max(logits, axis=-1, keepdims=True))
            total = jnp.sum(expd, axis=-1, keepdims=True)
            weighted = dot(expd.astype(BF16).reshape(256, 2048), values)
            result = (weighted.reshape(2, 128, HEAD) / total).astype(BF16)
            heads[part_of, z, :, pl.ds(pl.multiple_of(i * 256, 128), 256)] = jnp.concatenate(
                [result[0], result[1]], axis=1
            )
            return carry

        lax.fori_loop(0, 2, body, 0)

    def send_heads(i, k, a, rows_of, device):
        view = heads.at[i, a, rows_of]
        return send(view, view, h_s.at[i, k], h_r.at[i, k], device)

    moves = []
    for i in range(2):
        attend(i)
        moves.append([send_heads(i, k, z, pl.ds(0, 128), device) for k, device in enumerate((zp, zm))])
    for load in loads[1:]:
        load.start()
    send_down = send(down_ref.at[0, :, sib_half], wd.at[core_cols], pre_s.at[2], pre_r.at[2], sib)
    loads[0].wait()
    send_w_sib.wait_recv()

    order = [(h, a) for h in (xh, 1 - xh) for a in (z, down_z, up_z, far_z)]
    to_y = [None] * 8
    to_x = [None] * 8
    to_block = [None] * 8
    x_first = (2, 3, 5, 6)

    def project(*turns):
        side = order[turns[0]][0]
        side_cols = pl.ds(pl.multiple_of(side * 768, 128), 768)
        product = 0.0
        for i in range(2):
            lhs = jnp.concatenate([heads[i, order[t][1]] for t in turns], axis=0)
            product += dot(lhs, wcat[i * 512 : (i + 1) * 512, side_cols])
        for n, t in enumerate(turns):
            b = order[t]
            proj[*b] = product[n * 128 : (n + 1) * 128].astype(BF16).reshape(4, 2, 16, 768)
            if t in x_first:
                to_x[t] = send(
                    proj.at[*b, :, 1 - xl], got_pair.at[*b], x_s.at[t], x_r.at[t],
                    dev(z, xh, None, y * 2 + 1 - xl),
                )
                continue
            to_y[t] = [
                send(proj.at[*b, c], got_y.at[*b, y], y_s.at[t, j], y_r.at[t, j], dev(z, xh, None, c * 2 + xl))
                for j, c in enumerate(columns)
            ]
            got_y[*b, y] = proj[*b, y]

    def add_first(*turns):
        for t in turns:
            b = order[t]
            if t in x_first:
                to_x[t].wait_recv()
                pair_sum[*b] = (f32(proj[*b, :, xl]) + f32(got_pair[*b])).astype(BF16)
                to_y[t] = [
                    send(
                        pair_sum.at[*b, c], got_y.at[*b, y, 0], y_s.at[t, j], y_r.at[t, j],
                        dev(z, xh, None, c * 2 + xl),
                    )
                    for j, c in enumerate(columns)
                ]
                got_y[*b, y, 0] = pair_sum[*b, y]
                continue
            for copy in to_y[t]:
                copy.wait_recv()
            sums[*b] = jnp.sum(f32(got_y[*b]), axis=0)
            half_sum[*b] = sums[*b, 1 - xl].astype(BF16)
            to_x[t] = send(
                half_sum.at[*b], got_x.at[*b], x_s.at[t], x_r.at[t], dev(z, xh, None, y * 2 + 1 - xl)
            )

    def add_second(*turns):
        for t in turns:
            b = order[t]
            if t in x_first:
                for copy in to_y[t]:
                    copy.wait_recv()
                total = jnp.sum(f32(got_y[*b, :, 0]), axis=0).astype(BF16)
            else:
                to_x[t].wait_recv()
                total = (sums[*b, xl] + f32(got_x[*b])).astype(BF16)
            if t % 4 == 0:
                blocks[b[0], z] = total
            else:
                summed[*b] = total
                to_block[t] = send(
                    summed.at[*b], blocks.at[b[0], z], b_s.at[t], b_r.at[t], dev(b[1], xh)
                )

    project(0)
    far_w = []
    for i in range(4):
        send_w[i].wait_recv()
        view = wcat.at[pl.ds(i * piece, piece), proj_cols(1 - xh, core)]
        far_w.append(send(view, view, w_s.at[4 + i], w_r.at[4 + i], sib))
    for i in range(2):
        moves[i][0].wait_recv()
        moves[i].append(send_heads(i, 2, down_z, pl.ds(0, 64), zp))
        moves[i][1].wait_recv()
        moves[i].append(send_heads(i, 3, up_z, pl.ds(64, 64), zm))
    project(1, 2)
    for copy in far_w:
        copy.wait_recv()
    project(4, 5, 6)
    add_first(0, 1, 2)
    for i in range(2):
        moves[i][2].wait_recv()
        moves[i][3].wait_recv()
    project(3)
    project(7)
    add_second(0, 1)
    add_first(4, 5)
    add_second(2)
    add_first(6, 3)
    add_second(4, 5)
    add_first(7)
    add_second(6, 3, 7)
    for copy in to_block:
        if copy is not None:
            copy.wait_recv()
    square = jnp.zeros((16, 1), F32)
    for b in range(8):
        cols = slice(b * 768, (b + 1) * 768)
        attended = (f32(stream_ref[:, cols]) + f32(blocks[b % 2, b // 2])).astype(BF16)
        att_ref[:, cols] = attended
        square += jnp.sum(f32(attended) * f32(attended), axis=-1, keepdims=True)
    normed = f32(att_ref[...]) * lax.rsqrt(square / (2 * half) + 1e-05) * gain_ref[...]
    nrm[0] = normed[:, :half].astype(BF16)
    nrm[1] = normed[:, half:].astype(BF16)
    send_nrm = send(nrm.at[1 - core], nsib, pre_s.at[3], pre_r.at[3], sib)
    send_nrm.wait_recv()

    dispatches = [None] * NC
    shares = [[] for _ in range(NC)]

    def dispatch(c):
        half_of, start, width = UNITS[c]
        cols = pl.ds(start, width)
        slots = slice(half_of * 64, half_of * 64 + 64)
        picked = dot(match_own[slots], nrm[core, :, cols]) + dot(match_sib[slots], nsib[:, cols])
        disp[c][...] = picked.astype(BF16).reshape(4, 16, width)
        dispatches[c] = [
            send(
                disp[c].at[j], rows[c].at[own, j], disp_s.at[c, j], disp_r.at[c, j],
                dev(z, xh, None, lax.rem(exp + half_of * 4 + j, 8)),
            )
            for j in range(4)
            if half_of * 4 + j > 0
        ]
        if half_of == 0:
            rows[c][own, 0] = disp[c][0]

    def row_view(c):
        def view(block, piece):
            if piece is None:
                return rows[c].at[block]
            return rows[c].at[block, pl.ds(piece * 2, 2)]

        return view

    gather = [spread(row_view(c), ga_s.at[c], ga_r.at[c]) for c in range(NC)]

    def share(c, a):
        j = len(shares[c])
        pair = pl.ds(a * 2, 2)
        shares[c].append(send(rows[c].at[pair], rows_sib[c].at[pair], sib_s.at[c, j], sib_r.at[c, j], sib))

    def gather_a(c):
        for copy in dispatches[c]:
            copy.wait_recv()
        gather[c][0]()

    def gather_b(c):
        gather[c][1]()
        share(c, z)

    def gather_c(c):
        gather[c][2]()

    def gather_d(c):
        gather[c][3]()
        share(c, down_z)
        share(c, up_z)
        share(c, far_z)

    def term(source, c, base, i):
        _, start, width = UNITS[c]
        lhs = source[c][pl.ds(i * 4, 4)].reshape(256, width)
        return dot(lhs, wgu[pl.ds(pl.multiple_of(base + start, 128), width), :])

    def multiply_own(c):
        if c == 0:
            loads[1].wait()
            loads[2].wait()
        half_of, start, _ = UNITS[c]

        def body(i, carry):
            value = term(rows, c, core * half, i)
            acc[half_of, i] = value if start == 0 else acc[half_of, i] + value
            return carry

        lax.fori_loop(0, 2, body, 0)

    sent_hidden = [[], []]

    def multiply_sib(c):
        for copy in shares[c]:
            copy.wait_recv()
        half_of, start, width = UNITS[c]

        def body(i, carry):
            acc[half_of, i] += term(rows_sib, c, (1 - core) * half, i)
            return carry

        if start + width < half:
            lax.fori_loop(0, 2, body, 0)
            return
        for i in range(2):
            value = acc[half_of, i] + term(rows_sib, c, (1 - core) * half, i)
            gate_part, up_part = value[:, :384], value[:, 384:]
            hid[half_of, i, :, core_cols] = (gate_part / (1.0 + jnp.exp(-gate_part)) * up_part).astype(BF16)
            view = hid.at[half_of, i, :, core_cols]
            sent_hidden[half_of].append(
                send(view, view, hid_s.at[half_of, i], hid_r.at[half_of, i], sib)
            )

    reduce = [[None] * 8 for _ in range(NC)]
    returns = [None] * NC

    def send_sum(c, k, src, dst, device):
        reduce[c][k] = send(src, dst, rs_s.at[c, k], rs_r.at[c, k], device)

    def reduce_a(c):
        half_of, start, width = UNITS[c]

        def body(i, carry):
            out = dot(hid[half_of, i], wd[:, start : start + width])
            part[c][pl.ds(i * 4, 4)] = out.astype(BF16).reshape(4, 4, 16, width)
            return carry

        if c == 0:
            loads[3].wait()
            send_down.wait_recv()
        if start == 0:
            for i in range(2):
                sent_hidden[half_of][i].wait_recv()
                body(i, 0)
        else:
            lax.fori_loop(0, 2, body, 0)
        send_sum(c, 0, part[c].at[blk(up_z, 1 - xh)], got1[c].at[0], zp)
        send_sum(c, 1, part[c].at[blk(down_z, 1 - xh)], got1[c].at[1], zm)
        send_sum(c, 2, part[c].at[blk(far_z, 1 - xh)], got2[c], xp)

    def reduce_b(c):
        reduce[c][2].wait_recv()
        block = blk(far_z, xh)
        part[c][block] = (f32(part[c][block]) + f32(got2[c][...])).astype(BF16)
        send_sum(c, 3, part[c].at[block, pl.ds(0, 2)], got4[c].at[0], zm)
        send_sum(c, 4, part[c].at[block, pl.ds(2, 2)], got4[c].at[1], zp)
        reduce[c][0].wait_recv()
        reduce[c][1].wait_recv()
        block = blk(z, 1 - xh)
        part[c][block] = (f32(part[c][block]) + f32(got1[c][0]) + f32(got1[c][1])).astype(BF16)
        send_sum(c, 5, part[c].at[block], got3[c], xp)

    def reduce_c(c):
        reduce[c][3].wait_recv()
        block = blk(down_z, xh)
        part[c][block, 0:2] = (f32(part[c][block, 0:2]) + f32(got4[c][0])).astype(BF16)
        send_sum(c, 6, part[c].at[block], got5[c].at[0], zm)
        reduce[c][4].wait_recv()
        block = blk(up_z, xh)
        part[c][block, 2:4] = (f32(part[c][block, 2:4]) + f32(got4[c][1])).astype(BF16)
        send_sum(c, 7, part[c].at[block], got5[c].at[1], zp)

    def reduce_d(c):
        for k in (5, 6, 7):
            reduce[c][k].wait_recv()
        final[c][...] = (f32(part[c][own]) + f32(got3[c][...]) + (f32(got5[c][0]) + f32(got5[c][1]))).astype(BF16)
        half_of = UNITS[c][0]
        returns[c] = [
            send(
                final[c].at[j], back[c].at[j], back_s.at[c, j], back_r.at[c, j],
                dev(z, xh, None, lax.rem(exp + 8 - half_of * 4 - j, 8)),
            )
            for j in range(4)
            if half_of * 4 + j > 0
        ]
        if half_of == 0:
            back[c][0] = final[c][0]

    def weigh(weight, values):
        return jnp.dot(weight, values, precision=lax.Precision.HIGHEST, preferred_element_type=F32)

    def combine(c):
        for copy in returns[c]:
            copy.wait_recv()
        half_of, start, width = UNITS[c]
        values = f32(back[c][...].reshape(64, width))
        slots = slice(half_of * 64, half_of * 64 + 64)
        for_sib, for_own = weigh(weight_sib[:, slots], values), weigh(weight_own[:, slots], values)
        cols = slice(start, start + width)
        if half_of == 0:
            contrib_sib[:, cols] = for_sib
            contrib_own[:, cols] = for_own
            return
        contrib_sib[:, cols] += for_sib
        place = pl.ds(pl.multiple_of(core * half + start, 128), width)
        out_ref[:, place] = (f32(att_ref[:, place]) + (contrib_own[:, cols] + for_own)).astype(BF16)

    dispatch(0)
    dispatch(1)
    staged(
        NC,
        (0, gather_a),
        (-2, dispatch),
        (1, gather_b),
        (2, gather_c),
        (3, gather_d),
        (3, multiply_own),
        (4, multiply_sib),
        (FIRST + 3, reduce_a),
        (FIRST + 4, reduce_b),
        (FIRST + 5, reduce_c),
        (FIRST + 6, reduce_d),
        (FIRST + 7, combine),
    )

    last = send(contrib_sib, contrib, pre_s.at[4], pre_r.at[4], sib)
    last.wait_recv()
    out_ref[:, sib_half] = (f32(att_ref[:, sib_half]) + contrib[...]).astype(BF16)
    for copy in started:
        copy.wait_send()


def on_device(
    stream,
    queries,
    key_head_rows,
    value_head_rows,
    block_order,
    out_weight,
    norm_gain,
    gate_weight,
    up_weight,
    down_weight,
    expert_ids,
    expert_weights,
):
    d = stream.shape[1]
    half = d // 2
    vmem = pl.BlockSpec(memory_space=pltpu.VMEM)
    smem = pl.BlockSpec(memory_space=pltpu.SMEM)
    anyspace = pl.BlockSpec(memory_space=pl.ANY)

    def per_chunk(*shape):
        return [pltpu.VMEM(shape + (width,), BF16) for _, _, width in UNITS]

    def sems(*shapes):
        return [pltpu.SemaphoreType.DMA(shape) for shape in shapes for _ in range(2)]

    return pl.pallas_call(
        layer_kernel,
        out_shape=(jax.ShapeDtypeStruct(stream.shape, BF16),) * 2,
        in_specs=[vmem, vmem, vmem, smem, anyspace, vmem, vmem, vmem, vmem, anyspace, anyspace, anyspace],
        out_specs=(vmem, vmem),
        scratch_shapes=[
            pltpu.VMEM((2, 2, 4, 2, 128, 128), BF16),
            pltpu.VMEM((1, 2048), jnp.int32),
            pltpu.VMEM((128, 2048), F32),
            pltpu.VMEM((1024, 1536), BF16),
            pltpu.VMEM((2, 4, 128, 512), BF16),
            pltpu.VMEM((2, 4, 4, 2, 16, 768), BF16),
            pltpu.VMEM((2, 4, 4, 2, 16, 768), BF16),
            pltpu.VMEM((2, 4, 2, 16, 768), F32),
            pltpu.VMEM((2, 4, 16, 768), BF16),
            pltpu.VMEM((2, 4, 16, 768), BF16),
            pltpu.VMEM((2, 4, 4, 16, 768), BF16),
            pltpu.VMEM((2, 4, 4, 16, 768), BF16),
            pltpu.VMEM((2, 4, 16, 768), BF16),
            pltpu.VMEM((2, 4, 16, 768), BF16),
            pltpu.VMEM((d, 768), BF16),
            pltpu.VMEM((768, half), BF16),
            pltpu.VMEM((8, 128), F32),
            pltpu.VMEM((8, 128), F32),
            pltpu.VMEM((2, 16, half), BF16),
            pltpu.VMEM((16, half), BF16),
            per_chunk(4, 16),
            per_chunk(8, 4, 16),
            per_chunk(8, 4, 16),
            pltpu.VMEM((2, 2, 256, 768), F32),
            pltpu.VMEM((2, 2, 256, 768), BF16),
            per_chunk(8, 4, 16),
            per_chunk(2, 4, 16),
            per_chunk(4, 16),
            per_chunk(4, 16),
            per_chunk(2, 2, 16),
            per_chunk(2, 4, 16),
            per_chunk(4, 16),
            per_chunk(4, 16),
            pltpu.VMEM((16, half), F32),
            pltpu.VMEM((16, half), F32),
            pltpu.VMEM((16, half), F32),
            pltpu.SemaphoreType.DMA((4,)),
        ]
        + sems(
            (5,), (9,), (8,), (2, 4), (8, 3), (8,), (8,),
            (NC, 4), (NC, 8), (NC, 4), (2, 2), (NC, 8), (NC, 4),
        ),
        compiler_params=pltpu.CompilerParams(
            collective_id=0, has_side_effects=True, vmem_limit_bytes=VMEM_LIMIT
        ),
        cost_estimate=pl.CostEstimate(
            flops=2 * 3 * 1024 * d * 384 + 4 * 1024 * 128 * 2048 + 2 * 1024 * 1024 * 768,
            bytes_accessed=3 * d * 384 * 2,
            transcendentals=1024 * 2048 + 1024 * 384,
        ),
        name="layer",
    )(
        queries, key_head_rows, value_head_rows, block_order, out_weight, stream, norm_gain.reshape(1, d),
        expert_ids.T, expert_weights.T, gate_weight, up_weight, down_weight,
    )


def solution(mesh):
    in_specs = (
        P(("ctx", "exp"), None),
        P("ctx", "exp"),
        P("ctx", "exp"),
        P("ctx", "exp"),
        P(),
        P("exp", "ctx"),
        P(),
        P("exp", None, "ctx"),
        P("exp", None, "ctx"),
        P("exp", "ctx", None),
        P(("ctx", "exp"), None),
        P(("ctx", "exp"), None),
    )
    out_specs = (P(("ctx", "exp"), None), P(("ctx", "exp"), None))
    return jax.shard_map(
        on_device, mesh=mesh, in_specs=in_specs, out_specs=out_specs, check_vma=False
    )
```

```python
import jax
import jax.numpy as jnp
from jax import lax
from jax.experimental import pallas as pl
from jax.experimental.pallas import tpu as pltpu
from jax.sharding import PartitionSpec as P

HEAD = 128
MESH = pl.DeviceIdType.MESH
VMEM_LIMIT = 62 * 2**20
SPLITS = ((768, 768, 768, 768), (768, 768, 768, 768))
UNITS = tuple(
    (part, sum(split[:c]), width) for part, split in enumerate(SPLITS) for c, width in enumerate(split)
)
FIRST = len(SPLITS[0])
NC = len(UNITS)
BF16, F32 = jnp.bfloat16, jnp.float32


def f32(value):
    return value.astype(F32)


def dot(a, b):
    return jnp.dot(a, b, preferred_element_type=F32)


def remote(src, dst, send, recv, device):
    return pltpu.make_async_remote_copy(
        src_ref=src, dst_ref=dst, send_sem=send, recv_sem=recv, device_id=device, device_id_type=MESH
    )


def greet(devices):
    barrier = pltpu.get_barrier_semaphore()
    for device in devices:
        pl.semaphore_signal(barrier, inc=1, device_id=device, device_id_type=MESH)
    pl.semaphore_wait(barrier, len(devices))


def slot_match(meta, core, exp):
    row = lax.broadcasted_iota(jnp.int32, (128, 128), 0)
    lane = lax.broadcasted_iota(jnp.int32, (128, 128), 1)
    expert = f32(lax.rem(exp + row // 16, 8))
    first = (meta[0:1, :] == expert) & (lane < 16)
    second = (meta[1:2, :] == expert) & (lane < 16)
    named = jnp.where(first | second, 1.0, 0.0)
    earlier = jnp.where(row < lane, 1.0, 0.0)
    rank = dot(named.astype(BF16), earlier.astype(BF16))
    slot = f32(lax.rem(row, 8))
    mine = lax.rem(row // 8, 2) == core
    match = jnp.where((rank == slot) & mine, named, 0.0)
    weight = match * jnp.where(first, meta[2:3, :], meta[3:4, :])
    return match[:, :16].astype(BF16), weight.T[:16, :]


def staged(count, *stages):
    for step in range(count + max(late for late, _ in stages)):
        for late, stage in stages:
            if 0 <= step - late < count:
                stage(step - late)


def layer_kernel(
    q_ref, k_ref, v_ref, order_ref, proj_ref, stream_ref, gain_ref, ids_ref, mix_ref,
    gate_ref, up_ref, down_ref, att_ref, out_ref,
    kv, kpos, bias, wcat, heads, proj, got_y, sums, half_sum, got_x, got_pair, pair_sum, summed, blocks,
    wgu, wd, meta, meta_sib, nrm, nsib, disp, rows, rows_sib, acc, hid, part,
    got1, got2, got3, got4, got5, final, back, contrib, contrib_sib, contrib_own,
    load_sem, pre_s, pre_r, kv_s, kv_r, w_s, w_r, h_s, h_r, y_s, y_r, x_s, x_r, b_s, b_r,
    disp_s, disp_r, ga_s, ga_r, sib_s, sib_r, hid_s, hid_r, rs_s, rs_r, back_s, back_r, last_s, last_r,
):
    ctx = lax.axis_index("ctx")
    exp = lax.axis_index("exp")
    z, xh, core = ctx // 4, lax.rem(ctx // 2, 2), lax.rem(ctx, 2)
    y, xl = exp // 2, lax.rem(exp, 2)
    up_z, down_z, far_z = lax.rem(z + 1, 4), lax.rem(z + 3, 4), lax.rem(z + 2, 4)
    half = sum(SPLITS[0])

    def dev(a, b, c=None, e=None):
        return (a * 4 + b * 2 + (core if c is None else c), exp if e is None else e)

    def blk(a, b):
        return a * 2 + b

    zp, zm, xp, sib = dev(up_z, xh), dev(down_z, xh), dev(z, 1 - xh), dev(z, xh, 1 - core)
    peers = [lax.rem(exp + j, 8) for j in range(1, 8)]
    columns = [lax.rem(y + j, 4) for j in range(1, 4)]
    own = blk(z, xh)
    far = dev(far_z, xh)
    started = []

    def send(src, dst, s, r, device):
        copy = remote(src, dst, s, r, device)
        copy.start()
        started.append(copy)
        return copy

    def spread(view, s, r):
        copies = [None] * 8

        def forward(k, block, device, piece=None):
            ref = view(block, piece)
            copies[k] = send(ref, ref, s.at[k], r.at[k], device)

        def first():
            forward(0, own, zp)
            forward(1, own, zm)
            forward(2, own, xp)

        def second():
            copies[0].wait_recv()
            forward(3, blk(down_z, xh), zp, 0)
            copies[1].wait_recv()
            forward(4, blk(up_z, xh), zm, 1)
            copies[2].wait_recv()
            forward(5, blk(z, 1 - xh), zp)
            forward(6, blk(z, 1 - xh), zm)

        def third():
            copies[3].wait_recv()
            copies[4].wait_recv()
            forward(7, blk(far_z, xh), xp)

        def fourth():
            copies[5].wait_recv()
            copies[6].wait_recv()
            copies[7].wait_recv()

        return first, second, third, fourth

    def proj_cols(a, b):
        return pl.ds(pl.multiple_of((a * 2 + b) * 384, 128), 384)

    own_cols = proj_cols(xh, core)
    core_cols = pl.ds(pl.multiple_of(core * 384, 128), 384)
    core_half = pl.ds(pl.multiple_of(core * half, 128), half)
    sib_half = pl.ds(pl.multiple_of((1 - core) * half, 128), half)
    loads = [
        pltpu.make_async_copy(proj_ref, wcat.at[:, own_cols], load_sem.at[0]),
        pltpu.make_async_copy(gate_ref.at[0], wgu.at[:, pl.ds(0, 384)], load_sem.at[1]),
        pltpu.make_async_copy(up_ref.at[0], wgu.at[:, pl.ds(384, 384)], load_sem.at[2]),
        pltpu.make_async_copy(down_ref.at[0, :, core_half], wd.at[core_cols], load_sem.at[3]),
    ]
    loads[0].start()
    kv[core, xh, z, 0] = k_ref[...]
    kv[core, xh, z, 1] = v_ref[...]
    meta[...] = jnp.zeros_like(meta)
    meta[0:2, 0:16] = f32(ids_ref[...])
    meta[2:4, 0:16] = mix_ref[...]
    greet([zp, zm, far, xp, sib] + [dev(z, xh, None, e) for e in peers])

    def send_kv(k, a, b, device):
        return send(kv.at[core, a, b], kv.at[core, a, b], kv_s.at[k], kv_r.at[k], device)

    from_x = send_kv(0, xh, z, xp)
    column = [send_kv(1 + j, xh, z, device) for j, device in enumerate((zp, zm, far))]
    piece = 256
    send_w = [
        send(
            proj_ref.at[pl.ds(i * piece, piece)], wcat.at[pl.ds(i * piece, piece), own_cols],
            w_s.at[i], w_r.at[i], xp,
        )
        for i in range(4)
    ]
    send_w_sib = send(proj_ref, wcat.at[:, own_cols], pre_s.at[0], pre_r.at[0], sib)
    send_meta = send(meta, meta_sib, pre_s.at[1], pre_r.at[1], sib)
    from_x.wait_recv()
    column += [send_kv(4 + j, 1 - xh, z, device) for j, device in enumerate((zp, zm, far))]
    lane = lax.broadcasted_iota(jnp.int32, (1, 128), 1)
    for slot in range(16):
        place = slot % 4 * 4 + slot // 4 % 2 * 2 + slot // 8
        first = jnp.where(lane < 64, order_ref[2 * place], order_ref[2 * place + 1])
        kpos[:, slot * 128 : (slot + 1) * 128] = first * 64 + lax.rem(lane, 64)
    row = lax.broadcasted_iota(jnp.int32, (128, 1), 0)
    qpos = jnp.where(row < 64, order_ref[2 * ctx], order_ref[2 * ctx + 1]) * 64 + lax.rem(row, 64)
    bias[...] = jnp.where(kpos[...] <= qpos, 0.0, -1e30)
    match_own, weight_own = slot_match(meta[...], core, exp)
    for copy in column[:3]:
        copy.wait_recv()
    share_kv = [send(kv.at[core, xh], kv.at[core, xh], kv_s.at[7], kv_r.at[7], sib)]
    send_meta.wait_recv()
    match_sib, weight_sib = slot_match(meta_sib[...], 1 - core, exp)
    for copy in column[3:]:
        copy.wait_recv()
    share_kv.append(send(kv.at[core, 1 - xh], kv.at[core, 1 - xh], kv_s.at[8], kv_r.at[8], sib))
    for copy in share_kv:
        copy.wait_recv()

    scale = HEAD ** (-0.5) * 1.4426950408889634

    def attend(part_of):
        def body(i, carry):
            pair = q_ref[:, pl.ds(pl.multiple_of(part_of * 512 + i * 256, 128), 256)]
            q = jnp.concatenate([pair[:, :128], pair[:, 128:]], axis=0)
            keys = kv[:, :, :, 0].reshape(2048, HEAD)
            values = kv[:, :, :, 1].reshape(2048, HEAD)
            logits = lax.dot_general(q, keys, (((1,), (1,)), ((), ())), preferred_element_type=F32)
            logits = logits.reshape(2, 128, 2048) * scale + bias[...][None]
            expd = jnp.exp2(logits - jnp.max(logits, axis=-1, keepdims=True))
            total = jnp.sum(expd, axis=-1, keepdims=True)
            weighted = dot(expd.astype(BF16).reshape(256, 2048), values)
            result = (weighted.reshape(2, 128, HEAD) / total).astype(BF16)
            heads[part_of, z, :, pl.ds(pl.multiple_of(i * 256, 128), 256)] = jnp.concatenate(
                [result[0], result[1]], axis=1
            )
            return carry

        lax.fori_loop(0, 2, body, 0)

    def send_heads(i, k, a, rows_of, device):
        view = heads.at[i, a, rows_of]
        return send(view, view, h_s.at[i, k], h_r.at[i, k], device)

    moves = []
    for i in range(2):
        attend(i)
        moves.append([send_heads(i, k, z, pl.ds(0, 128), device) for k, device in enumerate((zp, zm))])
    for load in loads[1:]:
        load.start()
    send_down = send(down_ref.at[0, :, sib_half], wd.at[core_cols], pre_s.at[2], pre_r.at[2], sib)
    loads[0].wait()
    send_w_sib.wait_recv()

    order = [(h, a) for h in (xh, 1 - xh) for a in (z, down_z, up_z, far_z)]
    to_y = [None] * 8
    to_x = [None] * 8
    to_block = [None] * 8
    x_first = (2, 3, 5, 6)

    def project(*turns):
        side = order[turns[0]][0]
        side_cols = pl.ds(pl.multiple_of(side * 768, 128), 768)
        product = 0.0
        for i in range(2):
            lhs = jnp.concatenate([heads[i, order[t][1]] for t in turns], axis=0)
            product += dot(lhs, wcat[i * 512 : (i + 1) * 512, side_cols])
        for n, t in enumerate(turns):
            b = order[t]
            proj[*b] = product[n * 128 : (n + 1) * 128].astype(BF16).reshape(4, 2, 16, 768)
            if t in x_first:
                to_x[t] = send(
                    proj.at[*b, :, 1 - xl], got_pair.at[*b], x_s.at[t], x_r.at[t],
                    dev(z, xh, None, y * 2 + 1 - xl),
                )
                continue
            to_y[t] = [
                send(proj.at[*b, c], got_y.at[*b, y], y_s.at[t, j], y_r.at[t, j], dev(z, xh, None, c * 2 + xl))
                for j, c in enumerate(columns)
            ]
            got_y[*b, y] = proj[*b, y]

    def add_first(*turns):
        for t in turns:
            b = order[t]
            if t in x_first:
                to_x[t].wait_recv()
                pair_sum[*b] = (f32(proj[*b, :, xl]) + f32(got_pair[*b])).astype(BF16)
                to_y[t] = [
                    send(
                        pair_sum.at[*b, c], got_y.at[*b, y, 0], y_s.at[t, j], y_r.at[t, j],
                        dev(z, xh, None, c * 2 + xl),
                    )
                    for j, c in enumerate(columns)
                ]
                got_y[*b, y, 0] = pair_sum[*b, y]
                continue
            for copy in to_y[t]:
                copy.wait_recv()
            sums[*b] = jnp.sum(f32(got_y[*b]), axis=0)
            half_sum[*b] = sums[*b, 1 - xl].astype(BF16)
            to_x[t] = send(
                half_sum.at[*b], got_x.at[*b], x_s.at[t], x_r.at[t], dev(z, xh, None, y * 2 + 1 - xl)
            )

    def add_second(*turns):
        for t in turns:
            b = order[t]
            if t in x_first:
                for copy in to_y[t]:
                    copy.wait_recv()
                total = jnp.sum(f32(got_y[*b, :, 0]), axis=0).astype(BF16)
            else:
                to_x[t].wait_recv()
                total = (sums[*b, xl] + f32(got_x[*b])).astype(BF16)
            if t % 4 == 0:
                blocks[b[0], z] = total
            else:
                summed[*b] = total
                to_block[t] = send(
                    summed.at[*b], blocks.at[b[0], z], b_s.at[t], b_r.at[t], dev(b[1], xh)
                )

    project(0)
    far_w = []
    for i in range(4):
        send_w[i].wait_recv()
        view = wcat.at[pl.ds(i * piece, piece), proj_cols(1 - xh, core)]
        far_w.append(send(view, view, w_s.at[4 + i], w_r.at[4 + i], sib))
    for i in range(2):
        moves[i][0].wait_recv()
        moves[i].append(send_heads(i, 2, down_z, pl.ds(0, 64), zp))
        moves[i][1].wait_recv()
        moves[i].append(send_heads(i, 3, up_z, pl.ds(64, 64), zm))
    project(1, 2)
    for copy in far_w:
        copy.wait_recv()
    project(4, 5, 6)
    add_first(0, 1, 2)
    for i in range(2):
        moves[i][2].wait_recv()
        moves[i][3].wait_recv()
    project(3)
    project(7)
    add_second(0, 1)
    add_first(4, 5)
    add_second(2)
    add_first(6, 3)
    add_second(4, 5)
    add_first(7)
    add_second(6, 3, 7)
    for copy in to_block:
        if copy is not None:
            copy.wait_recv()
    square = jnp.zeros((16, 1), F32)
    for b in range(8):
        cols = slice(b * 768, (b + 1) * 768)
        attended = (f32(stream_ref[:, cols]) + f32(blocks[b % 2, b // 2])).astype(BF16)
        att_ref[:, cols] = attended
        square += jnp.sum(f32(attended) * f32(attended), axis=-1, keepdims=True)
    normed = f32(att_ref[...]) * lax.rsqrt(square / (2 * half) + 1e-05) * gain_ref[...]
    nrm[0] = normed[:, :half].astype(BF16)
    nrm[1] = normed[:, half:].astype(BF16)
    send_nrm = send(nrm.at[1 - core], nsib, pre_s.at[3], pre_r.at[3], sib)
    send_nrm.wait_recv()

    dispatches = [None] * NC
    shares = [[] for _ in range(NC)]

    def dispatch(c):
        half_of, start, width = UNITS[c]
        cols = pl.ds(start, width)
        slots = slice(half_of * 64, half_of * 64 + 64)
        picked = dot(match_own[slots], nrm[core, :, cols]) + dot(match_sib[slots], nsib[:, cols])
        disp[c][...] = picked.astype(BF16).reshape(4, 16, width)
        dispatches[c] = [
            send(
                disp[c].at[j], rows[c].at[own, j], disp_s.at[c, j], disp_r.at[c, j],
                dev(z, xh, None, lax.rem(exp + half_of * 4 + j, 8)),
            )
            for j in range(4)
            if half_of * 4 + j > 0
        ]
        if half_of == 0:
            rows[c][own, 0] = disp[c][0]

    def row_view(c):
        def view(block, piece):
            if piece is None:
                return rows[c].at[block]
            return rows[c].at[block, pl.ds(piece * 2, 2)]

        return view

    gather = [spread(row_view(c), ga_s.at[c], ga_r.at[c]) for c in range(NC)]

    def share(c, a):
        j = len(shares[c])
        pair = pl.ds(a * 2, 2)
        shares[c].append(send(rows[c].at[pair], rows_sib[c].at[pair], sib_s.at[c, j], sib_r.at[c, j], sib))

    def gather_a(c):
        for copy in dispatches[c]:
            copy.wait_recv()
        gather[c][0]()

    def gather_b(c):
        gather[c][1]()
        share(c, z)

    def gather_c(c):
        gather[c][2]()

    def gather_d(c):
        gather[c][3]()
        share(c, down_z)
        share(c, up_z)
        share(c, far_z)

    def term(source, c, base, i):
        _, start, width = UNITS[c]
        lhs = source[c][pl.ds(i * 4, 4)].reshape(256, width)
        return dot(lhs, wgu[pl.ds(pl.multiple_of(base + start, 128), width), :])

    sent_hidden = [[], []]

    def both(c, i):
        return term(rows, c, core * half, i) + term(rows_sib, c, (1 - core) * half, i)

    def multiply(c):
        if c == 0:
            loads[1].wait()
            loads[2].wait()
        for copy in shares[c]:
            copy.wait_recv()
        half_of, start, width = UNITS[c]

        def body(i, carry):
            acc[half_of, i] = both(c, i) if start == 0 else acc[half_of, i] + both(c, i)
            return carry

        if start + width < half:
            lax.fori_loop(0, 2, body, 0)
            return
        for i in range(2):
            value = acc[half_of, i] + both(c, i)
            gate_part, up_part = value[:, :384], value[:, 384:]
            hid[half_of, i, :, core_cols] = (gate_part / (1.0 + jnp.exp(-gate_part)) * up_part).astype(BF16)
            view = hid.at[half_of, i, :, core_cols]
            sent_hidden[half_of].append(
                send(view, view, hid_s.at[half_of, i], hid_r.at[half_of, i], sib)
            )

    reduce = [[None] * 8 for _ in range(NC)]
    returns = [None] * NC

    def send_sum(c, k, src, dst, device):
        reduce[c][k] = send(src, dst, rs_s.at[c, k], rs_r.at[c, k], device)

    def reduce_a(c):
        half_of, start, width = UNITS[c]

        def body(i, carry):
            out = dot(hid[half_of, i], wd[:, start : start + width])
            part[c][pl.ds(i * 4, 4)] = out.astype(BF16).reshape(4, 4, 16, width)
            return carry

        if c == 0:
            loads[3].wait()
            send_down.wait_recv()
        if start == 0:
            for i in range(2):
                sent_hidden[half_of][i].wait_recv()
                body(i, 0)
        else:
            lax.fori_loop(0, 2, body, 0)
        send_sum(c, 0, part[c].at[blk(up_z, 1 - xh)], got1[c].at[0], zp)
        send_sum(c, 1, part[c].at[blk(down_z, 1 - xh)], got1[c].at[1], zm)
        send_sum(c, 2, part[c].at[blk(far_z, 1 - xh)], got2[c], xp)

    def reduce_b(c):
        reduce[c][2].wait_recv()
        block = blk(far_z, xh)
        part[c][block] = (f32(part[c][block]) + f32(got2[c][...])).astype(BF16)
        send_sum(c, 3, part[c].at[block, pl.ds(0, 2)], got4[c].at[0], zm)
        send_sum(c, 4, part[c].at[block, pl.ds(2, 2)], got4[c].at[1], zp)
        reduce[c][0].wait_recv()
        reduce[c][1].wait_recv()
        block = blk(z, 1 - xh)
        part[c][block] = (f32(part[c][block]) + f32(got1[c][0]) + f32(got1[c][1])).astype(BF16)
        send_sum(c, 5, part[c].at[block], got3[c], xp)

    def reduce_c(c):
        reduce[c][3].wait_recv()
        block = blk(down_z, xh)
        part[c][block, 0:2] = (f32(part[c][block, 0:2]) + f32(got4[c][0])).astype(BF16)
        send_sum(c, 6, part[c].at[block], got5[c].at[0], zm)
        reduce[c][4].wait_recv()
        block = blk(up_z, xh)
        part[c][block, 2:4] = (f32(part[c][block, 2:4]) + f32(got4[c][1])).astype(BF16)
        send_sum(c, 7, part[c].at[block], got5[c].at[1], zp)

    def reduce_d(c):
        for k in (5, 6, 7):
            reduce[c][k].wait_recv()
        final[c][...] = (f32(part[c][own]) + f32(got3[c][...]) + (f32(got5[c][0]) + f32(got5[c][1]))).astype(BF16)
        half_of = UNITS[c][0]
        returns[c] = [
            send(
                final[c].at[j], back[c].at[j], back_s.at[c, j], back_r.at[c, j],
                dev(z, xh, None, lax.rem(exp + 8 - half_of * 4 - j, 8)),
            )
            for j in range(4)
            if half_of * 4 + j > 0
        ]
        if half_of == 0:
            back[c][0] = final[c][0]

    def weigh(weight, values):
        return jnp.dot(weight, values, precision=lax.Precision.HIGHEST, preferred_element_type=F32)

    lasts = []

    def combine(c):
        for copy in returns[c]:
            copy.wait_recv()
        half_of, start, width = UNITS[c]
        values = f32(back[c][...].reshape(64, width))
        slots = slice(half_of * 64, half_of * 64 + 64)
        for_sib, for_own = weigh(weight_sib[:, slots], values), weigh(weight_own[:, slots], values)
        cols = slice(start, start + width)
        if half_of == 0:
            contrib_sib[:, cols] = for_sib
            contrib_own[:, cols] = for_own
            return
        contrib_sib[:, cols] += for_sib
        n = c - FIRST
        view = pl.ds(start, width)
        lasts.append(send(contrib_sib.at[:, view], contrib.at[:, view], last_s.at[n], last_r.at[n], sib))
        place = pl.ds(pl.multiple_of(core * half + start, 128), width)
        out_ref[:, place] = (f32(att_ref[:, place]) + (contrib_own[:, cols] + for_own)).astype(BF16)

    def finish(c):
        if c < FIRST:
            return
        lasts[c - FIRST].wait_recv()
        _, start, width = UNITS[c]
        place = pl.ds(pl.multiple_of((1 - core) * half + start, 128), width)
        out_ref[:, place] = (f32(att_ref[:, place]) + contrib[:, start : start + width]).astype(BF16)

    dispatch(0)
    dispatch(1)
    staged(
        NC,
        (0, gather_a),
        (-2, dispatch),
        (1, gather_b),
        (2, gather_c),
        (3, gather_d),
        (4, multiply),
        (FIRST + 3, reduce_a),
        (FIRST + 4, reduce_b),
        (FIRST + 5, reduce_c),
        (FIRST + 6, reduce_d),
        (FIRST + 7, combine),
        (FIRST + 8, finish),
    )

    for copy in started:
        copy.wait_send()


def on_device(
    stream,
    queries,
    key_head_rows,
    value_head_rows,
    block_order,
    out_weight,
    norm_gain,
    gate_weight,
    up_weight,
    down_weight,
    expert_ids,
    expert_weights,
):
    d = stream.shape[1]
    half = d // 2
    vmem = pl.BlockSpec(memory_space=pltpu.VMEM)
    smem = pl.BlockSpec(memory_space=pltpu.SMEM)
    anyspace = pl.BlockSpec(memory_space=pl.ANY)

    def per_chunk(*shape):
        return [pltpu.VMEM(shape + (width,), BF16) for _, _, width in UNITS]

    def sems(*shapes):
        return [pltpu.SemaphoreType.DMA(shape) for shape in shapes for _ in range(2)]

    return pl.pallas_call(
        layer_kernel,
        out_shape=(jax.ShapeDtypeStruct(stream.shape, BF16),) * 2,
        in_specs=[vmem, vmem, vmem, smem, anyspace, vmem, vmem, vmem, vmem, anyspace, anyspace, anyspace],
        out_specs=(vmem, vmem),
        scratch_shapes=[
            pltpu.VMEM((2, 2, 4, 2, 128, 128), BF16),
            pltpu.VMEM((1, 2048), jnp.int32),
            pltpu.VMEM((128, 2048), F32),
            pltpu.VMEM((1024, 1536), BF16),
            pltpu.VMEM((2, 4, 128, 512), BF16),
            pltpu.VMEM((2, 4, 4, 2, 16, 768), BF16),
            pltpu.VMEM((2, 4, 4, 2, 16, 768), BF16),
            pltpu.VMEM((2, 4, 2, 16, 768), F32),
            pltpu.VMEM((2, 4, 16, 768), BF16),
            pltpu.VMEM((2, 4, 16, 768), BF16),
            pltpu.VMEM((2, 4, 4, 16, 768), BF16),
            pltpu.VMEM((2, 4, 4, 16, 768), BF16),
            pltpu.VMEM((2, 4, 16, 768), BF16),
            pltpu.VMEM((2, 4, 16, 768), BF16),
            pltpu.VMEM((d, 768), BF16),
            pltpu.VMEM((768, half), BF16),
            pltpu.VMEM((8, 128), F32),
            pltpu.VMEM((8, 128), F32),
            pltpu.VMEM((2, 16, half), BF16),
            pltpu.VMEM((16, half), BF16),
            per_chunk(4, 16),
            per_chunk(8, 4, 16),
            per_chunk(8, 4, 16),
            pltpu.VMEM((2, 2, 256, 768), F32),
            pltpu.VMEM((2, 2, 256, 768), BF16),
            per_chunk(8, 4, 16),
            per_chunk(2, 4, 16),
            per_chunk(4, 16),
            per_chunk(4, 16),
            per_chunk(2, 2, 16),
            per_chunk(2, 4, 16),
            per_chunk(4, 16),
            per_chunk(4, 16),
            pltpu.VMEM((16, half), F32),
            pltpu.VMEM((16, half), F32),
            pltpu.VMEM((16, half), F32),
            pltpu.SemaphoreType.DMA((4,)),
        ]
        + sems(
            (5,), (9,), (8,), (2, 4), (8, 3), (8,), (8,),
            (NC, 4), (NC, 8), (NC, 4), (2, 2), (NC, 8), (NC, 4), (NC - FIRST,),
        ),
        compiler_params=pltpu.CompilerParams(
            collective_id=0, has_side_effects=True, vmem_limit_bytes=VMEM_LIMIT
        ),
        cost_estimate=pl.CostEstimate(
            flops=2 * 3 * 1024 * d * 384 + 4 * 1024 * 128 * 2048 + 2 * 1024 * 1024 * 768,
            bytes_accessed=3 * d * 384 * 2,
            transcendentals=1024 * 2048 + 1024 * 384,
        ),
        name="layer",
    )(
        queries, key_head_rows, value_head_rows, block_order, out_weight, stream, norm_gain.reshape(1, d),
        expert_ids.T, expert_weights.T, gate_weight, up_weight, down_weight,
    )


def solution(mesh):
    in_specs = (
        P(("ctx", "exp"), None),
        P("ctx", "exp"),
        P("ctx", "exp"),
        P("ctx", "exp"),
        P(),
        P("exp", "ctx"),
        P(),
        P("exp", None, "ctx"),
        P("exp", None, "ctx"),
        P("exp", "ctx", None),
        P(("ctx", "exp"), None),
        P(("ctx", "exp"), None),
    )
    out_specs = (P(("ctx", "exp"), None), P(("ctx", "exp"), None))
    return jax.shard_map(
        on_device, mesh=mesh, in_specs=in_specs, out_specs=out_specs, check_vma=False
    )
```
